256 devices in a mesh: section: 4 (over y), shard: 64 (over z, x, core).
Axes of the slice: x: 4, y: 4, z: 8, core: 2. Of those that a mesh axis runs over, the one named last changes fastest.
Arguments:
- memory: bfloat16 [131072, 512], P('shard'), may hold values from -3 to 3
- last_time: int32 [131072], P('shard'), may hold values from 0 to 999
- requests: int32 [4, 64, 64, 1], P('section', 'shard'), may hold values from -1 to 255, as said below
- event_source: int32 [4, 16384], P('section', 'shard'), may hold values from 0 to 511, as said below
- event_target: int32 [4, 16384], P('section', 'shard'), may hold values from 0 to 511, as said below
- event_time: int32 [4, 16384], P('section', 'shard'), may hold values from 1000 to 4999, as said below
- neighbour_blocks: int32 [4, 16384, 4], P('section', 'shard'), may hold values from 0 to 63, as said below
- time_rates: float32 [128], replicated, may hold values from 0.001 to 1
- time_phase: float32 [128], replicated, may hold values from -3.140625 to 3.140625
- w_input: bfloat16 [1152, 1536], replicated, may hold values from -0.1875 to 0.1875
- w_hidden: bfloat16 [512, 1536], replicated, may hold values from -0.25 to 0.25
- bias_input: float32 [1536], replicated, may hold values from -3 to 3
- w_neighbour: bfloat16 [512, 512], replicated, may hold values from -0.25 to 0.25
Outputs:
- memory_after: bfloat16 [4, 131072, 512], P('section', 'shard')
- embeddings: bfloat16 [4, 16384, 512], P('section', 'shard')
The draws below stay inside these ranges and needn't reach their ends.
Inputs may be any that keep to these rules, and one draw needn't show every extreme that they name: `requests`: entry [b, j, o, c] is a block number among owner o's 256 blocks, or -1 for an empty slot; within one batch b each block of an owner is listed at most once among all devices; slot [b, j, j, 0] is never empty. `event_source`: events of device j in batch b name rows of blocks of non-empty slots [b, j, o, c]. `event_target`: events of device j in batch b name rows of blocks of non-empty slots [b, j, o, c]. `event_time`: times of batch b lie in [1000 (b + 1), 1000 (b + 2)). `neighbour_blocks`: positions of non-empty slots requested by the same device in the same batch.
All inputs are finite; a program needn't handle non-finite values.
Results may differ from the reference program's by a relative error of at most 0.004.
Values may be sent and summed in bfloat16 or wider, within the bound.
No kernel may reach another device: no remote copies, remote signals or barrier semaphores. Data moves between devices by JAX's collectives and lax.ppermute only.
A program may use at most 64 MiB of HBM per device.

```python
import math
import jax
import jax.numpy as jnp

M = 512
TE = 128
BR = 8
NB = 4
NODE_DEV = 2048
SLOTS = 64
EV = 256
NODES = 131072
BLK_DEV = 256
CAP = 1
MSG = 1152
N_SECTION = 4
N_SHARD = 64


def request_table(key):
    base_key = jax.random.fold_in(key, 11)
    perm_keys = jax.random.split(jax.random.fold_in(base_key, 1), N_SECTION * N_SHARD)
    slot_order = jax.vmap(lambda sub_key: jax.random.permutation(sub_key, SLOTS))(perm_keys).reshape(N_SECTION, N_SHARD, SLOTS).astype(jnp.int32)
    group_size = BLK_DEV // SLOTS
    offsets = jax.random.randint(jax.random.fold_in(base_key, 2), (N_SECTION, N_SHARD, SLOTS), 0, group_size)
    is_top = slot_order == SLOTS - 1
    offsets = jnp.where(is_top, group_size - 1, offsets)
    block_value = slot_order * group_size + offsets
    fill_level = jax.random.randint(jax.random.fold_in(base_key, 3), (N_SECTION, N_SHARD, 1), 1, 4)
    coin_flip = jax.random.randint(jax.random.fold_in(base_key, 4), (N_SECTION, N_SHARD, SLOTS), 0, 4)
    slot_iota = jnp.arange(SLOTS, dtype=jnp.int32)
    owner_iota = jnp.arange(N_SHARD, dtype=jnp.int32)
    own_slot = (slot_iota[None, :] == owner_iota[:, None] * CAP)[None]
    keep = (coin_flip < fill_level) | is_top | own_slot
    asked_blocks = jnp.where(keep, block_value, -1).reshape(N_SECTION, N_SHARD, N_SHARD, CAP)
    return jnp.transpose(asked_blocks, (0, 2, 1, 3)).astype(jnp.int32)


def live_slots(key):
    asked_blocks = request_table(key).reshape(N_SECTION, N_SHARD, SLOTS)
    is_live = (asked_blocks >= 0).astype(jnp.int32)
    live_order = jnp.argsort(1 - is_live, axis=-1, stable=True).astype(jnp.int32)
    return (live_order, is_live.sum(axis=-1))


def pick_blocks(key, salt, amount):
    live_order, live_count = live_slots(key)
    raw_draw = jax.random.randint(jax.random.fold_in(key, salt), (N_SECTION, N_SHARD, amount), 0, 1 << 20)
    chosen = raw_draw % live_count[..., None]
    return jnp.take_along_axis(live_order, chosen, axis=-1)


def draw_requests(key, part):
    return request_table(key)


def draw_event_source(key, part):
    blocks = pick_blocks(key, 21, EV)
    offsets = jax.random.randint(jax.random.fold_in(key, 22), (N_SECTION, N_SHARD, EV), 0, BR)
    return (blocks * BR + offsets).reshape(N_SECTION, N_SHARD * EV).astype(jnp.int32)


def draw_event_target(key, part):
    blocks = pick_blocks(key, 31, EV)
    offsets = jax.random.randint(jax.random.fold_in(key, 32), (N_SECTION, N_SHARD, EV), 0, BR)
    return (blocks * BR + offsets).reshape(N_SECTION, N_SHARD * EV).astype(jnp.int32)


def draw_neighbour_blocks(key, part):
    return pick_blocks(key, 41, EV * NB).reshape(N_SECTION, N_SHARD * EV, NB).astype(jnp.int32)


def draw_event_time(key, part):
    batch_iota = jnp.arange(N_SECTION, dtype=jnp.int32)[:, None]
    jitter = jax.random.randint(jax.random.fold_in(key, 51), (N_SECTION, N_SHARD * EV), 0, 1000)
    return (1000 * (batch_iota + 1) + jitter).astype(jnp.int32)


def plant(values, key, smallest, largest):
    longest = values.shape.index(max(values.shape))
    spots = []
    for shift in (0, 1):
        where = [jax.random.randint(jax.random.fold_in(key, axis), (), 0, length) for axis, length in enumerate(values.shape)]
        where[longest] = (where[longest] + shift) % values.shape[longest]
        spots.append(tuple(where))
    return values.at[spots[0]].set(smallest).at[spots[1]].set(largest)


def steps_of(key, extent, shards, low, top_value):
    level = 1.0
    for axis_at, blocks in shards:
        steps = jax.random.uniform(jax.random.fold_in(jax.random.fold_in(key, 6), axis_at), (blocks,), jnp.float32, low / len(shards), top_value / len(shards))
        level = level * jnp.repeat(jnp.exp(steps), extent[axis_at] // blocks).reshape((-1,) + (1,) * (len(extent) - 1 - axis_at))
    return level


def gaussian(stream_key, dims, spread, reach, pieces=(), held_as=jnp.bfloat16):
    result = spread * jax.random.normal(stream_key, dims, jnp.float32)
    if pieces:
        result = result * steps_of(stream_key, dims, pieces, -0.22, 0.18)
    return jnp.clip(result, -reach, reach).astype(held_as)


def setup_inputs(seed: int = 0) -> dict:
    streams_of = jax.random.split(jax.random.key(seed), 14)
    memory = gaussian(streams_of[0], (NODES, M), 0.5, 3.0, ((0, 64),))
    last_time = plant(jax.random.randint(streams_of[1], (NODES,), 0, 1000), jax.random.fold_in(streams_of[1], 1), 0, 999).astype(jnp.int32)
    requests = draw_requests(jax.random.fold_in(streams_of[13], 71), 0)
    event_source = draw_event_source(jax.random.fold_in(streams_of[13], 71), 0)
    event_target = draw_event_target(jax.random.fold_in(streams_of[13], 71), 0)
    event_time = draw_event_time(jax.random.fold_in(streams_of[13], 71), 0)
    neighbour_blocks = draw_neighbour_blocks(jax.random.fold_in(streams_of[13], 71), 0)
    time_rates = jnp.clip(jnp.exp(jax.random.uniform(streams_of[7], (TE,), jnp.float32, math.log(0.001), math.log(1.0))), 0.001, 1.0)
    time_phase = jnp.clip(jax.random.uniform(streams_of[8], (TE,), jnp.float32, -3.140625, 3.140625), -3.140625, 3.140625)
    w_input = gaussian(streams_of[9], (MSG, 3 * M), MSG ** -0.5, 0.1875)
    w_hidden = gaussian(streams_of[10], (M, 3 * M), M ** -0.5, 0.25)
    bias_input = gaussian(streams_of[11], (3 * M,), 0.5, 3.0, (), jnp.float32)
    w_neighbour = gaussian(streams_of[12], (M, M), M ** -0.5, 0.25)
    return {"memory": memory, "last_time": last_time, "requests": requests, "event_source": event_source, "event_target": event_target, "event_time": event_time, "neighbour_blocks": neighbour_blocks, "time_rates": time_rates, "time_phase": time_phase, "w_input": w_input, "w_hidden": w_hidden, "bias_input": bias_input, "w_neighbour": w_neighbour}


def time_code(delta, time_rates, time_phase):
    return jnp.cos(delta[..., None] * time_rates + time_phase)


def recur(averaged, states, w_input, w_hidden, bias_input):
    feat_width = states.shape[1]
    into = jnp.dot(averaged, w_input, preferred_element_type=jnp.float32) + bias_input
    carried = jnp.dot(states, w_hidden, preferred_element_type=jnp.float32)
    reset_gate = jax.nn.sigmoid(into[:, :feat_width] + carried[:, :feat_width])
    update_gate = jax.nn.sigmoid(into[:, feat_width:2 * feat_width] + carried[:, feat_width:2 * feat_width])
    candidate = jnp.tanh(into[:, 2 * feat_width:] + reset_gate * carried[:, 2 * feat_width:])
    return (1.0 - update_gate) * candidate + update_gate * states.astype(jnp.float32)


def reference(memory, last_time, requests, event_source, event_target, event_time, neighbour_blocks, time_rates, time_phase, w_input, w_hidden, bias_input, w_neighbour):
    slot_rows = SLOTS * BR
    total_slots = N_SHARD * slot_rows
    mem_table = memory
    stamps = last_time
    owner_iota = jnp.arange(N_SHARD, dtype=jnp.int32)
    row_iota = jnp.arange(BR, dtype=jnp.int32)
    device_base = (jnp.arange(N_SHARD, dtype=jnp.int32) * slot_rows)[:, None]
    snapshots = []
    embeddings = []
    for batch in range(N_SECTION):
        asked = requests[batch]
        is_live = jnp.broadcast_to((asked >= 0)[..., None], (N_SHARD, N_SHARD, CAP, BR)).reshape(N_SHARD, slot_rows)
        node_index = (owner_iota[None, :, None, None] * NODE_DEV + jnp.maximum(asked, 0)[..., None] * BR + row_iota).reshape(N_SHARD, slot_rows).astype(jnp.int32)
        pulled = jnp.where(is_live[..., None], mem_table[node_index], jnp.zeros((), jnp.bfloat16))
        pulled_time = jnp.where(is_live, stamps[node_index], 0).astype(jnp.int32)
        source = event_source[batch].reshape(N_SHARD, EV)
        target = event_target[batch].reshape(N_SHARD, EV)
        when = event_time[batch].reshape(N_SHARD, EV)
        src_states = jnp.take_along_axis(pulled, source[..., None], axis=1)
        dst_states = jnp.take_along_axis(pulled, target[..., None], axis=1)
        code_source = time_code((when - jnp.take_along_axis(pulled_time, source, axis=1)).astype(jnp.float32), time_rates, time_phase)
        code_target = time_code((when - jnp.take_along_axis(pulled_time, target, axis=1)).astype(jnp.float32), time_rates, time_phase)
        lead_msg = jnp.concatenate([src_states.astype(jnp.float32), dst_states.astype(jnp.float32), code_source], axis=-1)
        trail_msg = jnp.concatenate([dst_states.astype(jnp.float32), src_states.astype(jnp.float32), code_target], axis=-1)
        messages = jnp.concatenate([lead_msg.reshape(-1, MSG), trail_msg.reshape(-1, MSG)], axis=0)
        segment_ids = jnp.concatenate([(source + device_base).reshape(-1), (target + device_base).reshape(-1)]).astype(jnp.int32)
        summed = jax.ops.segment_sum(messages, segment_ids, num_segments=total_slots)
        counts = jax.ops.segment_sum(jnp.ones_like(segment_ids), segment_ids, num_segments=total_slots)
        both_times = jnp.concatenate([when.reshape(-1), when.reshape(-1)])
        latest = jax.ops.segment_max(both_times, segment_ids, num_segments=total_slots)
        averaged = (summed / jnp.maximum(counts, 1).astype(jnp.float32)[:, None]).astype(jnp.bfloat16)
        states = pulled.reshape(total_slots, M)
        new_states = recur(averaged, states, w_input, w_hidden, bias_input)
        updated = jnp.where(counts[:, None] > 0, new_states, states.astype(jnp.float32)).astype(jnp.bfloat16)
        new_time = jnp.where(counts > 0, latest, pulled_time.reshape(-1)).astype(jnp.int32)
        destination = jnp.where(is_live.reshape(-1), node_index.reshape(-1), NODE_DEV * N_SHARD).astype(jnp.int32)
        mem_table = mem_table.at[destination].set(updated, mode="drop")
        stamps = stamps.at[destination].set(new_time, mode="drop")
        snapshots.append(mem_table)
        block_means = pulled.reshape(N_SHARD, SLOTS, BR, M).astype(jnp.float32).mean(axis=2)
        neighbour_ids = neighbour_blocks[batch].reshape(N_SHARD, EV, NB)
        neighbour_sum = jax.vmap(lambda averages, chosen: averages[chosen].sum(axis=1))(block_means, neighbour_ids).astype(jnp.bfloat16)
        mixed = jnp.dot(neighbour_sum.reshape(-1, M), w_neighbour, preferred_element_type=jnp.float32)
        embedded = (src_states.reshape(-1, M).astype(jnp.float32) + mixed).astype(jnp.bfloat16)
        embeddings.append(embedded)
    return jnp.stack(snapshots), jnp.stack(embeddings)
```

```python
import functools

import jax
import jax.numpy as jnp
from jax import lax
from jax.experimental import pallas as pl
from jax.experimental.pallas import tpu as pltpu
from jax.sharding import PartitionSpec as P

BR = 8
NS = 4
LANES = 128
SLOTS = 64
ROWS = SLOTS * BR
EV = 256
BLOCKS = 256
M = 512
REQ = NS * BR
BF = jnp.bfloat16
F32 = jnp.float32
I32 = jnp.int32
VMEM = pltpu.VMEM
SMEM = pltpu.SMEM
NT = (((1,), (1,)), ((), ()))


def spec(space=VMEM):
    return pl.BlockSpec(memory_space=space)


def call(body, outs, ins, flops=0, moved=0, trans=0, scratch=()):
    return pl.pallas_call(
        body,
        out_shape=outs,
        in_specs=[spec(s) for s in ins],
        out_specs=jax.tree.map(lambda _: spec(), outs),
        scratch_shapes=list(scratch),
        compiler_params=pltpu.CompilerParams(vmem_limit_bytes=40 * 1024 * 1024),
        cost_estimate=pl.CostEstimate(flops=flops, bytes_accessed=moved, transcendentals=trans),
    )


def wide(rows, at):
    return jnp.concatenate([rows[at : at + 1, :], rows[at + 1 : at + 2, :]], axis=1)


def message_rows(rows):
    source, target, when = wide(rows, 0), wide(rows, 2), wide(rows, 4)
    return (
        jnp.concatenate([source, target], axis=1),
        jnp.concatenate([target, source], axis=1),
        jnp.concatenate([when, when], axis=1),
    )


def as_column(row):
    n = row.shape[1]
    eye = lax.broadcasted_iota(I32, (n, n), 0) == lax.broadcasted_iota(I32, (n, n), 1)
    return jnp.sum(jnp.where(eye, row, jnp.zeros_like(row)), axis=1, keepdims=True)


def events_kernel(sec_ref, ev_ref, pair_ref, pay_ref):
    sec = sec_ref[0]
    slot = lax.broadcasted_iota(I32, (ROWS, 2 * EV), 0)
    block = lax.broadcasted_iota(I32, (SLOTS, 2 * EV), 0)
    lane = lax.broadcasted_iota(I32, (SLOTS, LANES), 1)
    pay = jnp.zeros((SLOTS, LANES), I32)
    for b in range(NS):
        rows = ev_ref[lax.rem(b + NS - sec, NS)]
        to, other, when = message_rows(rows)
        hits = (slot == to).astype(F32).astype(BF)
        pairs = (slot == other).astype(F32).astype(BF)
        pair_ref[b] = lax.dot_general(hits, pairs, NT, preferred_element_type=F32).astype(BF)
        for r in range(BR):
            hit = block * BR + r == to
            latest = jnp.max(jnp.where(hit, when, 0), axis=1, keepdims=True)
            pay = jnp.where(lane == b * BR + r, latest, pay)
        asked = as_column(rows[6:7, 0:SLOTS])
        pay = jnp.where(lane == REQ + b, asked, pay)
    pay_ref[...] = pay


def owner_kernel(ids_ref, got_ref, last_ref, table_ref, out_ref):
    got = got_ref[...]
    flipped = jnp.transpose(
        jnp.concatenate([got.astype(F32), jnp.zeros((LANES - SLOTS, LANES), F32)], axis=0)
    ).astype(I32)
    cand = 4 * LANES
    lane = lax.broadcasted_iota(I32, (SLOTS, cand), 1)
    out_lane = lax.broadcasted_iota(I32, (SLOTS, LANES), 1)
    tail = jnp.zeros((1, SLOTS), I32)
    ids_row = jnp.concatenate(
        [lax.broadcasted_iota(I32, (1, BLOCKS), 1)]
        + [flipped[REQ + b : REQ + b + 1, 0:SLOTS] for b in range(NS - 1)]
        + [tail],
        axis=1,
    )
    times = [
        jnp.concatenate(
            [last_ref[r : r + 1, :]]
            + [flipped[b * BR + r : b * BR + r + 1, 0:SLOTS] for b in range(NS - 1)]
            + [tail],
            axis=1,
        )
        for r in range(BR)
    ]
    packed = jnp.zeros((SLOTS, LANES), I32)
    for b in range(NS):
        asked = got[:, REQ + b : REQ + b + 1]
        match = (asked == ids_row) & (asked >= 0) & (lane < BLOCKS + SLOTS * b)
        for r in range(BR):
            stamp = jnp.max(jnp.where(match, times[r], 0), axis=1, keepdims=True)
            packed = jnp.where(out_lane == b * BR + r, stamp >> 6, packed)
            packed = jnp.where(out_lane == REQ + b * BR + r, stamp & 63, packed)
    spread = jnp.broadcast_to(packed.astype(F32)[:, None, :], (SLOTS, BR, LANES))
    out_ref[:, :, LANES : 2 * LANES] = spread.astype(BF)
    for j in range(SLOTS):
        at = ids_ref[j, REQ]
        block = table_ref[jnp.maximum(at, 0)].astype(F32)
        out_ref[j, :, 0:LANES] = jnp.where(at >= 0, block, 0.0).astype(BF)


def swap_kernel(b, ids_ref, table_ref, back_ref, table_out, out_ref):
    table_out[...] = table_ref[...]
    for j in range(SLOTS):
        at = ids_ref[j, REQ + b]

        @pl.when(at >= 0)
        def _():
            table_out[jnp.maximum(at, 0)] = back_ref[j]

    for j in range(SLOTS):
        at = ids_ref[j, REQ + b + 1]
        block = table_out[jnp.maximum(at, 0)].astype(F32)
        out_ref[j] = jnp.where(at >= 0, block, 0.0).astype(BF)


def cosine(x):
    turns = jnp.round(x * 0.15915494309189535)
    x = x - turns * 6.28125
    x = x - turns * 0.0019340515136718750
    x = x - turns * 1.255665914e-06
    y = x * x
    total = jnp.full_like(y, -1.1470745597729725e-11)
    for c in (
        2.0876756987868099e-09,
        -2.7557319223985893e-07,
        2.4801587301587302e-05,
        -1.3888888888888889e-03,
        4.1666666666666667e-02,
        -0.5,
        1.0,
    ):
        total = total * y + c
    return total


def code_kernel(b, sec_ref, ev_ref, stamp_ref, rate_ref, phase_ref, out_ref):
    rows = ev_ref[lax.rem(b + NS - sec_ref[0], NS)]
    to, _, when = message_rows(rows)
    lane = lax.broadcasted_iota(I32, (ROWS, LANES), 1)
    sub = lax.broadcasted_iota(I32, (ROWS, LANES), 0) & (BR - 1)
    stamps = stamp_ref[:, LANES : 2 * LANES].astype(F32)
    scale = jnp.where(lane == b * BR + sub, 64.0, jnp.where(lane == REQ + b * BR + sub, 1.0, 0.0))
    state_time = jnp.sum(stamps * scale, axis=1, keepdims=True)
    hit = lax.broadcasted_iota(I32, (ROWS, 2 * EV), 0) == to
    before = jnp.sum(jnp.where(hit, state_time, 0.0), axis=0, keepdims=True)
    delta = when.astype(F32) - before
    code = cosine(as_column(rate_ref[...]) * delta + as_column(phase_ref[...]))
    high = code.astype(BF)
    low = (code - high.astype(F32)).astype(BF)
    hits = hit.astype(F32)
    counts = jnp.sum(hits, axis=1, keepdims=True)
    hits = hits.astype(BF)
    total = lax.dot_general(hits, high, NT, preferred_element_type=F32)
    total = total + lax.dot_general(hits, low, NT, preferred_element_type=F32)
    out_ref[...] = (total / jnp.maximum(counts, 1.0)).astype(BF)


def cell_kernel(
    b,
    sec_ref,
    own_ref,
    one_ref,
    two_ref,
    three_ref,
    pair_ref,
    code_ref,
    w_in_ref,
    w_hid_ref,
    bias_ref,
    new_ref,
    states_ref,
):
    sec = sec_ref[0]
    for k, part in enumerate((own_ref, one_ref, two_ref, three_ref)):
        at = pl.multiple_of(lax.rem(sec + k, NS) * LANES, LANES)
        states_ref[:, pl.ds(at, LANES)] = part[:, 0:LANES]
    states = states_ref[...]
    pairs = pair_ref[b]
    counts = jnp.sum(pairs.astype(F32), axis=1, keepdims=True)
    share = 1.0 / jnp.maximum(counts, 1.0)
    trail = (jnp.dot(pairs, states, preferred_element_type=F32) * share).astype(BF)
    into = jnp.dot(states, w_in_ref[0:M, :], preferred_element_type=F32)
    into = into + jnp.dot(trail, w_in_ref[M : 2 * M, :], preferred_element_type=F32)
    into = into + jnp.dot(code_ref[...], w_in_ref[2 * M :, :], preferred_element_type=F32)
    into = into + bias_ref[...]
    carried = jnp.dot(states, w_hid_ref[...], preferred_element_type=F32)
    gates = 0.5 + 0.5 * jnp.tanh(0.5 * (into[:, : 2 * LANES] + carried[:, : 2 * LANES]))
    reset, update = gates[:, :LANES], gates[:, LANES:]
    candidate = jnp.tanh(into[:, 2 * LANES :] + reset * carried[:, 2 * LANES :])
    old = own_ref[:, 0:LANES].astype(F32)
    new = (1.0 - update) * candidate + update * old
    new_ref[...] = jnp.where(counts > 0.0, new, old).astype(BF)


def final_kernel(sec_ref, ids_ref, mem_ref, *refs):
    early, late, out_ref = refs[:NS], refs[NS : 2 * NS], refs[2 * NS]
    sec = sec_ref[0]
    out_ref[...] = mem_ref[...]
    for b in range(NS):
        for j in range(SLOTS):
            at = ids_ref[j, REQ + b]

            @pl.when((at >= 0) & (sec >= b))
            def _():
                for k in range(NS):
                    to = pl.multiple_of(lax.rem(sec + k, NS) * LANES, LANES)
                    block = early[k][b, j] if b < NS - 1 else late[k][j]
                    out_ref[jnp.maximum(at, 0), :, pl.ds(to, LANES)] = block


def from_sections(array):
    return [array] + [
        lax.ppermute(array, "section", [(i, (i - k) % NS) for i in range(NS)]) for k in range(1, NS)
    ]


def exchange(array):
    return lax.all_to_all(array, "shard", split_axis=0, concat_axis=0, tiled=True)


def on_device(
    memory,
    last_time,
    requests,
    event_source,
    event_target,
    event_time,
    neighbour_blocks,
    time_rates,
    time_phase,
    w_input,
    w_hidden,
    bias_input,
    w_neighbour,
):
    sec = lax.axis_index("section")
    sec_ref = sec.astype(I32).reshape(1)
    source = event_source[0]
    ints = jnp.concatenate(
        [
            source,
            event_target[0],
            event_time[0],
            requests.reshape(SLOTS),
            jnp.zeros((8 * LANES - 3 * EV - SLOTS,), I32),
        ]
    ).reshape(8, LANES)
    events = jnp.stack(from_sections(ints))

    def quarter(array):
        rows = array.shape[0]
        return lax.dynamic_index_in_dim(
            array.reshape(rows, -1, NS, LANES), sec, axis=2, keepdims=False
        ).reshape(rows, -1)

    w_in = quarter(w_input)
    w_hid = quarter(w_hidden)
    bias = quarter(bias_input.reshape(1, -1))
    table = quarter(memory).reshape(BLOCKS, BR, LANES)
    last = last_time.reshape(BLOCKS, BR).T

    pairs, pay = call(
        events_kernel,
        (jax.ShapeDtypeStruct((NS, ROWS, ROWS), BF), jax.ShapeDtypeStruct((SLOTS, LANES), I32)),
        (SMEM, VMEM),
        flops=NS * 2 * ROWS**3,
        moved=NS * ROWS * ROWS * 2,
    )(sec_ref, events)
    ids = exchange(pay.reshape(SLOTS, 1, LANES)).reshape(SLOTS, LANES)
    picked = call(
        owner_kernel,
        jax.ShapeDtypeStruct((SLOTS, BR, 2 * LANES), BF),
        (SMEM, VMEM, VMEM, VMEM),
        flops=10**6,
        moved=10**6,
    )(ids, ids, last, table)
    stamps = None
    kept, backs = [], []
    for b in range(NS):
        pulled = exchange(picked).reshape(ROWS, -1)
        if b == 0:
            stamps = pulled
            pulled = pulled[:, :LANES]
        parts = from_sections(pulled)
        code = call(
            functools.partial(code_kernel, b),
            jax.ShapeDtypeStruct((ROWS, LANES), BF),
            (SMEM, VMEM, VMEM, VMEM, VMEM),
            flops=4 * ROWS * ROWS * LANES,
            moved=10**6,
            trans=ROWS * LANES,
        )(sec_ref, events, stamps, time_rates.reshape(1, LANES), time_phase.reshape(1, LANES))
        updated, states = call(
            functools.partial(cell_kernel, b),
            (jax.ShapeDtypeStruct((ROWS, LANES), BF), jax.ShapeDtypeStruct((ROWS, M), BF)),
            (SMEM,) + (VMEM,) * 9,
            flops=2 * ROWS * M * (M + 9 * LANES * 3 + M * 3),
            moved=4 * 10**6,
            trans=3 * ROWS * LANES,
        )(sec_ref, *parts, pairs, code, w_in, w_hid, bias)
        kept.append(states)
        back = exchange(updated.reshape(SLOTS, BR, LANES))
        backs.append(back)
        if b < NS - 1:
            table, picked = call(
                functools.partial(swap_kernel, b),
                (
                    jax.ShapeDtypeStruct((BLOCKS, BR, LANES), BF),
                    jax.ShapeDtypeStruct((SLOTS, BR, LANES), BF),
                ),
                (SMEM, VMEM, VMEM),
                flops=10**5,
                moved=10**6,
            )(ids, table, back)

    early = from_sections(jnp.stack(backs[:-1]))
    late = from_sections(backs[-1])
    final = call(
        final_kernel,
        jax.ShapeDtypeStruct((BLOCKS, BR, M), BF),
        (SMEM, SMEM) + (VMEM,) * 9,
        flops=10**5,
        moved=8 * 10**6,
    )(sec_ref, ids, memory.reshape(BLOCKS, BR, M), *early, *late)

    own = kept[0]
    for b in range(1, NS):
        own = jnp.where(sec == b, kept[b], own)
    block_of_slot = jnp.arange(ROWS, dtype=I32) // BR
    weight = (neighbour_blocks[0][:, :, None] == block_of_slot).astype(F32).sum(axis=1) * 0.125
    neighbour_sum = jnp.dot(weight.astype(BF), own, preferred_element_type=F32).astype(BF)
    mixed = jnp.dot(neighbour_sum, w_neighbour, preferred_element_type=F32)
    one_hot = (source[:, None] == jnp.arange(ROWS, dtype=I32)).astype(BF)
    embedded = (jnp.dot(one_hot, own, preferred_element_type=F32) + mixed).astype(BF)
    return (final.reshape(1, BLOCKS * BR, M), embedded[None])


def solution(mesh):
    return jax.shard_map(
        on_device,
        mesh=mesh,
        in_specs=(
            P("shard", None),
            P("shard"),
            P("section", "shard", None, None),
            P("section", "shard"),
            P("section", "shard"),
            P("section", "shard"),
            P("section", "shard", None),
            P(),
            P(),
            P(),
            P(),
            P(),
            P(),
        ),
        out_specs=(P("section", "shard", None), P("section", "shard", None)),
        check_vma=False,
    )
```

```python
import functools

import jax
import jax.numpy as jnp
from jax import lax
from jax.experimental import pallas as pl
from jax.experimental.pallas import tpu as pltpu
from jax.sharding import PartitionSpec as P

BR = 8
NS = 4
LANES = 128
SLOTS = 64
ROWS = SLOTS * BR
EV = 256
BLOCKS = 256
M = 512
PUT = NS * BR
GET = PUT + NS
BF = jnp.bfloat16
F32 = jnp.float32
I32 = jnp.int32
VMEM = pltpu.VMEM
SMEM = pltpu.SMEM
NT = (((1,), (1,)), ((), ()))


def spec(space=VMEM):
    return pl.BlockSpec(memory_space=space)


def call(body, outs, ins, to=None, scratch=(), flops=0, moved=0, aliases=None):
    return pl.pallas_call(
        body,
        out_shape=outs,
        in_specs=[spec(s) for s in ins],
        out_specs=jax.tree.map(lambda _: spec(), outs) if to is None else to,
        scratch_shapes=list(scratch),
        input_output_aliases=aliases or {},
        compiler_params=pltpu.CompilerParams(vmem_limit_bytes=16 * 1024 * 1024),
        cost_estimate=pl.CostEstimate(flops=flops, bytes_accessed=moved, transcendentals=0),
    )


def wide(rows, at):
    return jnp.concatenate([rows[at : at + 1, :], rows[at + 1 : at + 2, :]], axis=1)


def message_rows(rows):
    source, target, when = wide(rows, 0), wide(rows, 2), wide(rows, 4)
    return (
        jnp.concatenate([source, target], axis=1),
        jnp.concatenate([target, source], axis=1),
        jnp.concatenate([when, when], axis=1),
    )


def as_column(row):
    n = row.shape[1]
    eye = lax.broadcasted_iota(I32, (n, n), 0) == lax.broadcasted_iota(I32, (n, n), 1)
    return jnp.sum(jnp.where(eye, row, jnp.zeros_like(row)), axis=1, keepdims=True)


def prep_kernel(sec_ref, w_in_ref, w_hid_ref, bias_ref, mem_ref, in_out, hid_out, bias_out, table_out, sems):
    sec = sec_ref[0]
    column = pl.multiple_of(sec * LANES, LANES)
    copies = [
        pltpu.make_async_copy(
            mem_ref.at[:, :, pl.ds(column, LANES)], table_out.at[pl.ds(0, BLOCKS)], sems.at[6]
        )
    ]
    for g in range(3):
        column = pl.multiple_of(g * M + sec * LANES, LANES)
        for k, (src, dst) in enumerate(((w_in_ref, in_out), (w_hid_ref, hid_out))):
            copies.append(
                pltpu.make_async_copy(
                    src.at[:, pl.ds(column, LANES)],
                    dst.at[:, pl.ds(g * LANES, LANES)],
                    sems.at[2 * g + k],
                )
            )
        bias_out[:, g * LANES : (g + 1) * LANES] = bias_ref[:, pl.ds(column, LANES)]
    for copy in copies:
        copy.start()
    table_out[BLOCKS:] = jnp.zeros((8, BR, LANES), BF)
    for copy in copies:
        copy.wait()


def events_kernel(sec_ref, ev_ref, pay_ref):
    sec = sec_ref[0]
    block = lax.broadcasted_iota(I32, (SLOTS, 2 * EV), 0) * BR
    lane = lax.broadcasted_iota(I32, (SLOTS, LANES), 1)
    pay = jnp.zeros((SLOTS, LANES), I32)
    for b in range(NS):
        rows = ev_ref[lax.rem(b + NS - sec, NS)]
        to, _, when = message_rows(rows)
        place = to - block
        for r in range(BR):
            latest = jnp.max(jnp.where(place == r, when, 0), axis=1, keepdims=True)
            pay = jnp.where(lane == b * BR + r, latest, pay)
        asked = as_column(rows[6:7, 0:SLOTS])
        pay = jnp.where(lane == PUT + b, jnp.where(asked < 0, BLOCKS, asked), pay)
        pay = jnp.where(lane == GET + b, jnp.where(asked < 0, BLOCKS + 1, asked), pay)
    pay_ref[...] = pay


def owner_kernel(ids_ref, got_ref, last_ref, table_ref, out_ref):
    for j in range(SLOTS):
        out_ref[j, :, 0:LANES] = table_ref[ids_ref[j, GET]]
    got = got_ref[...]
    flipped = jnp.transpose(
        jnp.concatenate([got.astype(F32), jnp.zeros((LANES - SLOTS, LANES), F32)], axis=0)
    ).astype(I32)
    cand = BLOCKS + NS * SLOTS
    lane = lax.broadcasted_iota(I32, (SLOTS, cand), 1)
    group = lax.broadcasted_iota(I32, (SLOTS, LANES), 1) // BR
    ids_row = jnp.concatenate(
        [lax.broadcasted_iota(I32, (1, BLOCKS), 1)]
        + [flipped[PUT + b : PUT + b + 1, 0:SLOTS] for b in range(NS)],
        axis=1,
    )
    match = jnp.concatenate(
        [
            ((got[:, GET + b : GET + b + 1] == ids_row) & (lane < BLOCKS + SLOTS * b)).astype(F32)
            for b in range(NS)
        ],
        axis=0,
    ).astype(BF)
    base = jnp.concatenate(
        [jnp.zeros((BLOCKS, (NS - 1) * BR), I32), last_ref[...], jnp.zeros((BLOCKS, LANES - NS * BR), I32)],
        axis=1,
    )
    times = jnp.concatenate(
        [base] + [jnp.where(group == b, got, 0) for b in range(NS - 1)] + [jnp.zeros((SLOTS, LANES), I32)],
        axis=0,
    )
    high = jnp.dot(match, (times >> 6).astype(F32).astype(BF), preferred_element_type=F32)
    low = jnp.dot(match, (times & 63).astype(F32).astype(BF), preferred_element_type=F32)
    stamp = high * 64.0 + low
    stamp = jnp.maximum(stamp, pltpu.roll(stamp, LANES - 2 * BR, 1))
    stamp = jnp.maximum(stamp, pltpu.roll(stamp, LANES - BR, 1)).astype(I32)
    total = jnp.zeros((SLOTS, LANES), I32)
    for b in range(NS):
        part = stamp[b * SLOTS : (b + 1) * SLOTS]
        part = pltpu.roll(part, b * BR, 1) if b else part
        total = jnp.where(group == b, part, total)
    packed = (total >> 6) + pltpu.roll(total & 63, PUT, 1)
    spread = jnp.broadcast_to(packed.astype(F32)[:, None, :], (SLOTS, BR, LANES))
    out_ref[:, :, LANES : 2 * LANES] = spread.astype(BF)


def swap_kernel(b, ids_ref, table_ref, back_ref, table_out, out_ref):
    table_out[...] = table_ref[...]
    for j in range(SLOTS):
        table_out[ids_ref[j, PUT + b]] = back_ref[j]
    for j in range(SLOTS):
        out_ref[j] = table_out[ids_ref[j, GET + b + 1]]


def cosine(x):
    turns = jnp.round(x * 0.15915494309189535)
    x = x - turns * 6.28125
    x = x - turns * 0.0019340515136718750
    x = x - turns * 1.255665914e-06
    y = x * x
    total = jnp.full_like(y, -1.1470745597729725e-11)
    for c in (
        2.0876756987868099e-09,
        -2.7557319223985893e-07,
        2.4801587301587302e-05,
        -1.3888888888888889e-03,
        4.1666666666666667e-02,
        -0.5,
        1.0,
    ):
        total = total * y + c
    return total


def code_kernel(b, sec_ref, ev_ref, stamp_ref, rate_ref, phase_ref, out_ref, pair_ref):
    rows = ev_ref[lax.rem(b + NS - sec_ref[0], NS)]
    to, other, when = message_rows(rows)
    lane = lax.broadcasted_iota(I32, (ROWS, LANES), 1)
    sub = lax.broadcasted_iota(I32, (ROWS, LANES), 0) & (BR - 1)
    stamps = stamp_ref[:, LANES : 2 * LANES].astype(F32)
    scale = jnp.where(lane == b * BR + sub, 64.0, jnp.where(lane == PUT + b * BR + sub, 1.0, 0.0))
    state_time = jnp.sum(stamps * scale, axis=1, keepdims=True)
    slot = lax.broadcasted_iota(I32, (ROWS, 2 * EV), 0)
    hit = slot == to
    before = jnp.sum(jnp.where(hit, state_time, 0.0), axis=0, keepdims=True)
    delta = when.astype(F32) - before
    code = cosine(as_column(rate_ref[...]) * delta + as_column(phase_ref[...]))
    high = code.astype(BF)
    low = (code - high.astype(F32)).astype(BF)
    hits = hit.astype(F32)
    counts = jnp.sum(hits, axis=1, keepdims=True)
    hits = hits.astype(BF)
    total = lax.dot_general(hits, high, NT, preferred_element_type=F32)
    total = total + lax.dot_general(hits, low, NT, preferred_element_type=F32)
    out_ref[...] = (total / jnp.maximum(counts, 1.0)).astype(BF)
    partner = (slot == other).astype(F32).astype(BF)
    pair_ref[...] = lax.dot_general(hits, partner, NT, preferred_element_type=F32).astype(BF)


def cell_kernel(
    b,
    sec_ref,
    own_ref,
    one_ref,
    two_ref,
    three_ref,
    pair_ref,
    code_ref,
    w_in_ref,
    w_hid_ref,
    bias_ref,
    *refs,
):
    new_ref, kept_ref, states_ref, sem = refs[-4:]
    sec = sec_ref[0]
    for k, part in enumerate((own_ref, one_ref, two_ref, three_ref)):
        at = pl.multiple_of(lax.rem(sec + k, NS) * LANES, LANES)
        states_ref[:, pl.ds(at, LANES)] = part[...]
    keep = pltpu.make_async_copy(states_ref, kept_ref, sem)

    @pl.when(sec == b)
    def _():
        keep.start()

    states = states_ref[...]
    pairs = pair_ref[...]
    counts = jnp.sum(pairs.astype(F32), axis=1, keepdims=True)
    share = 1.0 / jnp.maximum(counts, 1.0)
    trail = (jnp.dot(pairs, states, preferred_element_type=F32) * share).astype(BF)
    into = jnp.dot(states, w_in_ref[0:M, :], preferred_element_type=F32)
    into = into + jnp.dot(trail, w_in_ref[M : 2 * M, :], preferred_element_type=F32)
    into = into + jnp.dot(code_ref[...], w_in_ref[2 * M :, :], preferred_element_type=F32)
    into = into + bias_ref[...]
    carried = jnp.dot(states, w_hid_ref[...], preferred_element_type=F32)
    gates = 0.5 + 0.5 * jnp.tanh(0.5 * (into[:, : 2 * LANES] + carried[:, : 2 * LANES]))
    reset, update = gates[:, :LANES], gates[:, LANES:]
    candidate = jnp.tanh(into[:, 2 * LANES :] + reset * carried[:, 2 * LANES :])
    old = own_ref[...].astype(F32)
    new = (1.0 - update) * candidate + update * old
    new_ref[...] = jnp.where(counts > 0.0, new, old).astype(BF)

    @pl.when(sec == b)
    def _():
        keep.wait()


def early_kernel(sec_ref, ids_ref, mem_ref, own_ref, one_ref, two_ref, three_ref, out_ref, full_ref, sem):
    sec = sec_ref[0]
    fill = pltpu.make_async_copy(mem_ref, full_ref.at[pl.ds(0, BLOCKS)], sem)
    fill.start()
    fill.wait()
    for b in range(NS - 1):

        @pl.when(sec >= b)
        def _():
            for k, part in enumerate((own_ref, one_ref, two_ref, three_ref)):
                to = pl.multiple_of(lax.rem(sec + k, NS) * LANES, LANES)
                for j in range(SLOTS):
                    full_ref[ids_ref[j, PUT + b], :, pl.ds(to, LANES)] = part[b, j]

    drain = pltpu.make_async_copy(full_ref.at[pl.ds(0, BLOCKS)], out_ref, sem)
    drain.start()
    drain.wait()


def late_kernel(sec_ref, ids_ref, zero_ref, one_ref, two_ref, own_ref, early_ref, out_ref, full_ref, sems):
    @pl.when(sec_ref[0] == NS - 1)
    def _():
        for k, part in enumerate((zero_ref, one_ref, two_ref, own_ref)):
            full_ref[:, :, k * LANES : (k + 1) * LANES] = part[...]

        def place(j):
            at = ids_ref[j, PUT + NS - 1]
            return at, pltpu.make_async_copy(
                full_ref.at[j], out_ref.at[jnp.minimum(at, BLOCKS - 1)], sems.at[j]
            )

        for j in range(SLOTS):
            at, copy = place(j)

            @pl.when(at < BLOCKS)
            def _():
                copy.start()

        for j in range(SLOTS):
            at, copy = place(j)

            @pl.when(at < BLOCKS)
            def _():
                copy.wait()


def from_sections(array):
    return [array] + [
        lax.ppermute(array, "section", [(i, (i - k) % NS) for i in range(NS)]) for k in range(1, NS)
    ]


def exchange(array):
    return lax.all_to_all(array, "shard", split_axis=0, concat_axis=0, tiled=True)


def on_device(
    memory,
    last_time,
    requests,
    event_source,
    event_target,
    event_time,
    neighbour_blocks,
    time_rates,
    time_phase,
    w_input,
    w_hidden,
    bias_input,
    w_neighbour,
):
    sec = lax.axis_index("section")
    sec_ref = sec.astype(I32).reshape(1)
    source = event_source[0]
    ints = jnp.concatenate(
        [
            source,
            event_target[0],
            event_time[0],
            requests.reshape(SLOTS),
            jnp.zeros((8 * LANES - 3 * EV - SLOTS,), I32),
        ]
    ).reshape(8, LANES)
    events = jnp.stack(from_sections(ints))
    w_in, w_hid, bias, table = call(
        prep_kernel,
        (
            jax.ShapeDtypeStruct((w_input.shape[0], 3 * LANES), BF),
            jax.ShapeDtypeStruct((M, 3 * LANES), BF),
            jax.ShapeDtypeStruct((1, 3 * LANES), F32),
            jax.ShapeDtypeStruct((BLOCKS + 8, BR, LANES), BF),
        ),
        (SMEM, pl.ANY, pl.ANY, VMEM, pl.ANY),
        scratch=(pltpu.SemaphoreType.DMA((7,)),),
        moved=4 * 10**6,
    )(sec_ref, w_input, w_hidden, bias_input.reshape(1, -1), memory.reshape(BLOCKS, BR, M))

    pay = call(
        events_kernel, jax.ShapeDtypeStruct((SLOTS, LANES), I32), (SMEM, VMEM), moved=10**6
    )(sec_ref, events)
    ids = exchange(pay.reshape(SLOTS, 1, LANES)).reshape(SLOTS, LANES)
    picked = call(
        owner_kernel,
        jax.ShapeDtypeStruct((SLOTS, BR, 2 * LANES), BF),
        (SMEM, VMEM, VMEM, VMEM),
        moved=10**6,
    )(ids, ids, last_time.reshape(BLOCKS, BR), table)
    stamps = kept = None
    backs = []
    for b in range(NS):
        pulled = exchange(picked).reshape(ROWS, -1)
        if b == 0:
            stamps = pulled
            pulled = pulled[:, :LANES]
        parts = from_sections(pulled)
        code, pairs = call(
            functools.partial(code_kernel, b),
            (jax.ShapeDtypeStruct((ROWS, LANES), BF), jax.ShapeDtypeStruct((ROWS, ROWS), BF)),
            (SMEM, VMEM, VMEM, VMEM, VMEM),
            flops=2 * ROWS**3,
            moved=10**6,
        )(sec_ref, events, stamps, time_rates.reshape(1, LANES), time_phase.reshape(1, LANES))
        updated, kept = call(
            functools.partial(cell_kernel, b),
            (jax.ShapeDtypeStruct((ROWS, LANES), BF), jax.ShapeDtypeStruct((ROWS, M), BF)),
            (SMEM,) + (VMEM,) * 9 + ((pl.ANY,) if b else ()),
            to=(spec(), spec(pl.ANY)),
            scratch=(pltpu.VMEM((ROWS, M), BF), pltpu.SemaphoreType.DMA),
            flops=2 * ROWS * M * (M + 9 * LANES),
            moved=4 * 10**6,
            aliases={10: 1} if b else None,
        )(sec_ref, *parts, pairs, code, w_in, w_hid, bias, *([kept] if b else []))
        updated = updated.reshape(SLOTS, BR, LANES)
        if b == NS - 1:
            updated, backs = lax.optimization_barrier((updated, backs))
            early = from_sections(jnp.stack(backs))
        back = exchange(updated)
        if b < NS - 1:
            backs.append(back)
            table, picked = call(
                functools.partial(swap_kernel, b),
                (
                    jax.ShapeDtypeStruct((BLOCKS + 8, BR, LANES), BF),
                    jax.ShapeDtypeStruct((SLOTS, BR, LANES), BF),
                ),
                (SMEM, VMEM, VMEM),
                moved=10**6,
            )(ids, table, back)

    full = jax.ShapeDtypeStruct((BLOCKS, BR, M), BF)
    final = call(
        early_kernel,
        full,
        (SMEM, SMEM, pl.ANY) + (VMEM,) * NS,
        to=spec(pl.ANY),
        scratch=(pltpu.VMEM((BLOCKS + 8, BR, M), BF), pltpu.SemaphoreType.DMA),
        moved=8 * 10**6,
    )(sec_ref, ids, memory.reshape(BLOCKS, BR, M), *early)
    late = [lax.ppermute(back, "section", [(k, NS - 1)]) for k in range(NS - 1)]
    final = call(
        late_kernel,
        full,
        (SMEM, SMEM) + (VMEM,) * NS + (pl.ANY,),
        to=spec(pl.ANY),
        scratch=(pltpu.VMEM((SLOTS, BR, M), BF), pltpu.SemaphoreType.DMA((SLOTS,))),
        moved=10**6,
        aliases={6: 0},
    )(sec_ref, ids, *late, back, final)

    own = kept
    block_of_slot = jnp.arange(ROWS, dtype=I32) // BR
    weight = (neighbour_blocks[0][:, :, None] == block_of_slot).astype(F32).sum(axis=1) * 0.125
    neighbour_sum = jnp.dot(weight.astype(BF), own, preferred_element_type=F32).astype(BF)
    mixed = jnp.dot(neighbour_sum, w_neighbour, preferred_element_type=F32)
    one_hot = (source[:, None] == jnp.arange(ROWS, dtype=I32)).astype(BF)
    embedded = (jnp.dot(one_hot, own, preferred_element_type=F32) + mixed).astype(BF)
    return (final.reshape(1, BLOCKS * BR, M), embedded[None])


def solution(mesh):
    return jax.shard_map(
        on_device,
        mesh=mesh,
        in_specs=(
            P("shard", None),
            P("shard"),
            P("section", "shard", None, None),
            P("section", "shard"),
            P("section", "shard"),
            P("section", "shard"),
            P("section", "shard", None),
            P(),
            P(),
            P(),
            P(),
            P(),
            P(),
        ),
        out_specs=(P("section", "shard", None), P("section", "shard", None)),
        check_vma=False,
    )
```

```python
import functools

import jax
import jax.numpy as jnp
from jax import lax
from jax.experimental import pallas as pl
from jax.experimental.pallas import tpu as pltpu
from jax.sharding import PartitionSpec as P

BR = 8
NS = 4
LANES = 128
SLOTS = 64
ROWS = SLOTS * BR
EV = 256
BLOCKS = 256
M = 512
PUT = NS * BR
GET = PUT + NS
BF = jnp.bfloat16
F32 = jnp.float32
I32 = jnp.int32
VMEM = pltpu.VMEM
SMEM = pltpu.SMEM
HBM = pltpu.HBM
NT = (((1,), (1,)), ((), ()))


def spec(space=VMEM):
    return pl.BlockSpec(memory_space=space)


def call(body, outs, ins, to=None, scratch=(), flops=0, moved=0, aliases=None, mib=16):
    return pl.pallas_call(
        body,
        out_shape=outs,
        in_specs=[spec(s) for s in ins],
        out_specs=jax.tree.map(lambda _: spec(), outs) if to is None else to,
        scratch_shapes=list(scratch),
        input_output_aliases=aliases or {},
        compiler_params=pltpu.CompilerParams(vmem_limit_bytes=mib * 1024 * 1024),
        cost_estimate=pl.CostEstimate(flops=flops, bytes_accessed=moved, transcendentals=0),
    )


def wide(rows, at):
    return jnp.concatenate([rows[at : at + 1, :], rows[at + 1 : at + 2, :]], axis=1)


def message_rows(rows):
    source, target, when = wide(rows, 0), wide(rows, 2), wide(rows, 4)
    return (
        jnp.concatenate([source, target], axis=1),
        jnp.concatenate([target, source], axis=1),
        jnp.concatenate([when, when], axis=1),
    )


def as_column(row):
    n = row.shape[1]
    eye = lax.broadcasted_iota(I32, (n, n), 0) == lax.broadcasted_iota(I32, (n, n), 1)
    return jnp.sum(jnp.where(eye, row, jnp.zeros_like(row)), axis=1, keepdims=True)


def prep_kernel(sec_ref, w_in_ref, w_hid_ref, bias_ref, in_out, hid_out, bias_out):
    for g in range(3):
        column = pl.multiple_of(g * M + sec_ref[0] * LANES, LANES)
        for src, dst in ((w_in_ref, in_out), (w_hid_ref, hid_out), (bias_ref, bias_out)):
            dst[:, g * LANES : (g + 1) * LANES] = src[:, pl.ds(column, LANES)]


def events_kernel(sec_ref, ev_ref, pay_ref):
    sec = sec_ref[0]
    block = lax.broadcasted_iota(I32, (SLOTS, 2 * EV), 0) * BR
    lane = lax.broadcasted_iota(I32, (SLOTS, LANES), 1)
    pay = jnp.zeros((SLOTS, LANES), I32)
    for b in range(NS):
        rows = ev_ref[lax.rem(b + NS - sec, NS)]
        to, _, when = message_rows(rows)
        place = to - block
        for r in range(BR):
            latest = jnp.max(jnp.where(place == r, when, 0), axis=1, keepdims=True)
            pay = jnp.where(lane == b * BR + r, latest, pay)
        asked = as_column(rows[6:7, 0:SLOTS])
        pay = jnp.where(lane == PUT + b, jnp.where(asked < 0, BLOCKS, asked), pay)
        pay = jnp.where(lane == GET + b, jnp.where(asked < 0, BLOCKS + 1, asked), pay)
    pay_ref[...] = pay


def owner_kernel(ids_ref, got_ref, last_ref, table_ref, out_ref, rows_ref, table_out):
    table_out[:BLOCKS] = table_ref[...]
    table_out[BLOCKS:] = jnp.zeros((8, BR, LANES), BF)
    for j in range(SLOTS):
        out_ref[j, :, 0:LANES] = table_out[ids_ref[j, GET]]
    got = got_ref[...]
    flipped = jnp.transpose(
        jnp.concatenate([got.astype(F32), jnp.zeros((LANES - SLOTS, LANES), F32)], axis=0)
    ).astype(I32)
    rows_ref[...] = flipped[PUT : PUT + 2 * NS, :]
    cand = BLOCKS + NS * SLOTS
    lane = lax.broadcasted_iota(I32, (SLOTS, cand), 1)
    group = lax.broadcasted_iota(I32, (SLOTS, LANES), 1) // BR
    ids_row = jnp.concatenate(
        [lax.broadcasted_iota(I32, (1, BLOCKS), 1)]
        + [flipped[PUT + b : PUT + b + 1, 0:SLOTS] for b in range(NS)],
        axis=1,
    )
    match = jnp.concatenate(
        [
            ((got[:, GET + b : GET + b + 1] == ids_row) & (lane < BLOCKS + SLOTS * b)).astype(F32)
            for b in range(NS)
        ],
        axis=0,
    ).astype(BF)
    base = jnp.concatenate(
        [jnp.zeros((BLOCKS, (NS - 1) * BR), I32), last_ref[...], jnp.zeros((BLOCKS, LANES - NS * BR), I32)],
        axis=1,
    )
    times = jnp.concatenate(
        [base] + [jnp.where(group == b, got, 0) for b in range(NS - 1)] + [jnp.zeros((SLOTS, LANES), I32)],
        axis=0,
    )
    high = jnp.dot(match, (times >> 6).astype(F32).astype(BF), preferred_element_type=F32)
    low = jnp.dot(match, (times & 63).astype(F32).astype(BF), preferred_element_type=F32)
    stamp = high * 64.0 + low
    stamp = jnp.maximum(stamp, pltpu.roll(stamp, LANES - 2 * BR, 1))
    stamp = jnp.maximum(stamp, pltpu.roll(stamp, LANES - BR, 1)).astype(I32)
    total = jnp.zeros((SLOTS, LANES), I32)
    for b in range(NS):
        part = stamp[b * SLOTS : (b + 1) * SLOTS]
        part = pltpu.roll(part, b * BR, 1) if b else part
        total = jnp.where(group == b, part, total)
    packed = (total >> 6) + pltpu.roll(total & 63, PUT, 1)
    spread = jnp.broadcast_to(packed.astype(F32)[:, None, :], (SLOTS, BR, LANES))
    out_ref[:, :, LANES : 2 * LANES] = spread.astype(BF)


def swap_kernel(b, ids_ref, table_ref, back_ref, out_ref, table_out):
    table_out[...] = table_ref[...]
    for j in range(SLOTS):
        table_out[ids_ref[b, j]] = back_ref[j]
    for j in range(SLOTS):
        out_ref[j] = table_out[ids_ref[NS + b + 1, j]]


def cosine(x):
    turns = jnp.round(x * 0.15915494309189535)
    x = x - turns * 6.28125
    x = x - turns * 0.0019340515136718750
    x = x - turns * 1.255665914e-06
    y = x * x
    total = jnp.full_like(y, -1.1470745597729725e-11)
    for c in (
        2.0876756987868099e-09,
        -2.7557319223985893e-07,
        2.4801587301587302e-05,
        -1.3888888888888889e-03,
        4.1666666666666667e-02,
        -0.5,
        1.0,
    ):
        total = total * y + c
    return total


def code_kernel(b, sec_ref, ev_ref, stamp_ref, rate_ref, phase_ref, out_ref, pair_ref):
    rows = ev_ref[lax.rem(b + NS - sec_ref[0], NS)]
    to, other, when = message_rows(rows)
    lane = lax.broadcasted_iota(I32, (ROWS, LANES), 1)
    sub = lax.broadcasted_iota(I32, (ROWS, LANES), 0) & (BR - 1)
    stamps = stamp_ref[:, LANES : 2 * LANES].astype(F32)
    scale = jnp.where(lane == b * BR + sub, 64.0, jnp.where(lane == PUT + b * BR + sub, 1.0, 0.0))
    state_time = jnp.sum(stamps * scale, axis=1, keepdims=True)
    slot = lax.broadcasted_iota(I32, (ROWS, 2 * EV), 0)
    hit = slot == to
    before = jnp.sum(jnp.where(hit, state_time, 0.0), axis=0, keepdims=True)
    delta = when.astype(F32) - before
    code = cosine(as_column(rate_ref[...]) * delta + as_column(phase_ref[...]))
    high = code.astype(BF)
    low = (code - high.astype(F32)).astype(BF)
    hits = hit.astype(F32)
    counts = jnp.sum(hits, axis=1, keepdims=True)
    hits = hits.astype(BF)
    total = lax.dot_general(hits, high, NT, preferred_element_type=F32)
    total = total + lax.dot_general(hits, low, NT, preferred_element_type=F32)
    out_ref[...] = (total / jnp.maximum(counts, 1.0)).astype(BF)
    partner = (slot == other).astype(F32).astype(BF)
    pair_ref[...] = lax.dot_general(hits, partner, NT, preferred_element_type=F32).astype(BF)


def cell_kernel(
    b,
    sec_ref,
    own_ref,
    one_ref,
    two_ref,
    three_ref,
    pair_ref,
    code_ref,
    w_in_ref,
    w_hid_ref,
    bias_ref,
    *refs,
):
    new_ref, kept_ref, states_ref, sem = refs[-4:]
    sec = sec_ref[0]
    for k, part in enumerate((own_ref, one_ref, two_ref, three_ref)):
        at = pl.multiple_of(lax.rem(sec + k, NS) * LANES, LANES)
        states_ref[:, pl.ds(at, LANES)] = part[...]
    keep = pltpu.make_async_copy(states_ref, kept_ref, sem)

    @pl.when(sec == b)
    def _():
        keep.start()

    states = states_ref[...]
    pairs = pair_ref[...]
    counts = jnp.sum(pairs.astype(F32), axis=1, keepdims=True)
    share = 1.0 / jnp.maximum(counts, 1.0)
    trail = (jnp.dot(pairs, states, preferred_element_type=F32) * share).astype(BF)
    into = jnp.dot(states, w_in_ref[0:M, :], preferred_element_type=F32)
    into = into + jnp.dot(trail, w_in_ref[M : 2 * M, :], preferred_element_type=F32)
    into = into + jnp.dot(code_ref[...], w_in_ref[2 * M :, :], preferred_element_type=F32)
    into = into + bias_ref[...]
    carried = jnp.dot(states, w_hid_ref[...], preferred_element_type=F32)
    gates = 0.5 + 0.5 * jnp.tanh(0.5 * (into[:, : 2 * LANES] + carried[:, : 2 * LANES]))
    reset, update = gates[:, :LANES], gates[:, LANES:]
    candidate = jnp.tanh(into[:, 2 * LANES :] + reset * carried[:, 2 * LANES :])
    old = own_ref[...].astype(F32)
    new = (1.0 - update) * candidate + update * old
    new_ref[...] = jnp.where(counts > 0.0, new, old).astype(BF)

    @pl.when(sec == b)
    def _():
        keep.wait()


def early_kernel(sec_ref, ids_ref, mem_ref, own_ref, one_ref, two_ref, three_ref, out_ref, full_ref, sem):
    sec = sec_ref[0]
    fill = pltpu.make_async_copy(mem_ref, full_ref.at[pl.ds(0, BLOCKS)], sem)
    fill.start()
    fill.wait()
    for b in range(NS - 1):

        @pl.when(sec >= b)
        def _():
            for k, part in enumerate((own_ref, one_ref, two_ref, three_ref)):
                to = pl.multiple_of(lax.rem(sec + k, NS) * LANES, LANES)
                for j in range(SLOTS):
                    full_ref[ids_ref[b, j], :, pl.ds(to, LANES)] = part[b, j]

    drain = pltpu.make_async_copy(full_ref.at[pl.ds(0, BLOCKS)], out_ref, sem)
    drain.start()
    drain.wait()


def late_kernel(sec_ref, ids_ref, zero_ref, one_ref, two_ref, own_ref, early_ref, out_ref, full_ref, sems):
    @pl.when(sec_ref[0] == NS - 1)
    def _():
        for k, part in enumerate((zero_ref, one_ref, two_ref, own_ref)):
            full_ref[:, :, k * LANES : (k + 1) * LANES] = part[...]

        def place(j):
            at = ids_ref[NS - 1, j]
            return at, pltpu.make_async_copy(
                full_ref.at[j], out_ref.at[jnp.minimum(at, BLOCKS - 1)], sems.at[j]
            )

        for j in range(SLOTS):
            at, copy = place(j)

            @pl.when(at < BLOCKS)
            def _():
                copy.start()

        for j in range(SLOTS):
            at, copy = place(j)

            @pl.when(at < BLOCKS)
            def _():
                copy.wait()


def embed_kernel(source_ref, near_ref, kept_ref, weight_ref, out_ref):
    slot = lax.broadcasted_iota(I32, (EV, ROWS), 1)
    block = slot >> 3
    picks = jnp.zeros((EV, ROWS), F32)
    for k in range(near_ref.shape[0]):
        picks = picks + jnp.where(block == as_column(near_ref[k : k + 1, :]), 1.0 / BR, 0.0)
    states = kept_ref[...]
    near = jnp.dot(picks.astype(BF), states, preferred_element_type=F32).astype(BF)
    mixed = jnp.dot(near, weight_ref[...], preferred_element_type=F32)
    own = (slot == as_column(source_ref[...])).astype(F32).astype(BF)
    out_ref[...] = (jnp.dot(own, states, preferred_element_type=F32) + mixed).astype(BF)


def from_sections(array):
    return [array] + [
        lax.ppermute(array, "section", [(i, (i - k) % NS) for i in range(NS)]) for k in range(1, NS)
    ]


def exchange(array):
    return lax.all_to_all(array, "shard", split_axis=0, concat_axis=0, tiled=True)


def on_device(
    memory,
    last_time,
    requests,
    event_source,
    event_target,
    event_time,
    neighbour_blocks,
    time_rates,
    time_phase,
    w_input,
    w_hidden,
    bias_input,
    w_neighbour,
):
    sec = lax.axis_index("section")
    sec_ref = sec.astype(I32).reshape(1)
    source = event_source[0]
    ints = jnp.concatenate(
        [
            source,
            event_target[0],
            event_time[0],
            requests.reshape(SLOTS),
            jnp.zeros((8 * LANES - 3 * EV - SLOTS,), I32),
        ]
    ).reshape(8, LANES)
    parts = from_sections(ints)
    table = lax.dynamic_slice_in_dim(memory, sec * LANES, LANES, axis=1)
    last = last_time.reshape(BLOCKS, BR)
    bias_row = bias_input.reshape(1, -1)
    parts, table, last, bias_row = lax.optimization_barrier((parts, table, last, bias_row))
    events = jnp.stack(parts)
    pay = call(
        events_kernel, jax.ShapeDtypeStruct((SLOTS, LANES), I32), (SMEM, VMEM), moved=10**6
    )(sec_ref, events)
    ids = exchange(pay.reshape(SLOTS, 1, LANES)).reshape(SLOTS, LANES)
    picked, ids, table = call(
        owner_kernel,
        (
            jax.ShapeDtypeStruct((SLOTS, BR, 2 * LANES), BF),
            jax.ShapeDtypeStruct((2 * NS, LANES), I32),
            jax.ShapeDtypeStruct((BLOCKS + 8, BR, LANES), BF),
        ),
        (SMEM, VMEM, VMEM, VMEM),
        moved=10**6,
    )(ids, ids, last, table.reshape(BLOCKS, BR, LANES))
    stamps = kept = None
    backs = []
    for b in range(NS):
        pulled = exchange(picked).reshape(ROWS, -1)
        if b == 0:
            stamps = pulled
            pulled = pulled[:, :LANES]
            pulled, later = lax.optimization_barrier((pulled, sec_ref))
            w_in, w_hid, bias = call(
                prep_kernel,
                (
                    jax.ShapeDtypeStruct((w_input.shape[0], 3 * LANES), BF),
                    jax.ShapeDtypeStruct((M, 3 * LANES), BF),
                    jax.ShapeDtypeStruct((1, 3 * LANES), F32),
                ),
                (SMEM, VMEM, VMEM, VMEM),
                moved=3 * 10**6,
            )(later, w_input, w_hidden, bias_row)
        if b == NS - 1:
            early = from_sections(jnp.stack(backs))
            pulled, early = lax.optimization_barrier((pulled, early))
        parts = from_sections(pulled)
        if b == NS - 1:
            full = jax.ShapeDtypeStruct((BLOCKS, BR, M), BF)
            final = call(
                early_kernel,
                full,
                (SMEM, SMEM, pl.ANY) + (VMEM,) * NS,
                to=spec(pl.ANY),
                scratch=(pltpu.VMEM((BLOCKS + 8, BR, M), BF), pltpu.SemaphoreType.DMA),
                moved=8 * 10**6,
            )(sec_ref, ids, memory.reshape(BLOCKS, BR, M), *early)
            parts, final = lax.optimization_barrier((parts, final))
        code, pairs = call(
            functools.partial(code_kernel, b),
            (jax.ShapeDtypeStruct((ROWS, LANES), BF), jax.ShapeDtypeStruct((ROWS, ROWS), BF)),
            (SMEM, VMEM, VMEM, VMEM, VMEM),
            flops=2 * ROWS**3,
            moved=10**6,
        )(sec_ref, events, stamps, time_rates.reshape(1, LANES), time_phase.reshape(1, LANES))
        updated, kept = call(
            functools.partial(cell_kernel, b),
            (jax.ShapeDtypeStruct((ROWS, LANES), BF), jax.ShapeDtypeStruct((ROWS, M), BF)),
            (SMEM,) + (VMEM,) * 9 + ((pl.ANY,) if b else ()),
            to=(spec(), spec(pl.ANY)),
            scratch=(pltpu.VMEM((ROWS, M), BF), pltpu.SemaphoreType.DMA),
            flops=2 * ROWS * M * (M + 9 * LANES),
            moved=4 * 10**6,
            aliases={10: 1} if b else None,
        )(sec_ref, *parts, pairs, code, w_in, w_hid, bias, *([kept] if b else []))
        updated = updated.reshape(SLOTS, BR, LANES)
        if b == NS - 1:
            updated, near, source = lax.optimization_barrier(
                (updated, neighbour_blocks[0].T, source)
            )
        back = exchange(updated)
        if b < NS - 1:
            backs.append(back)
            block = jax.ShapeDtypeStruct((SLOTS, BR, LANES), BF)
            whole = (BLOCKS + 8, BR, LANES)
            if b < NS - 2:
                picked, table = call(
                    functools.partial(swap_kernel, b),
                    (block, jax.ShapeDtypeStruct(whole, BF)),
                    (SMEM, VMEM, VMEM),
                    moved=10**6,
                )(ids, table, back)
            else:
                picked = call(
                    functools.partial(swap_kernel, b),
                    block,
                    (SMEM, VMEM, VMEM),
                    scratch=(pltpu.VMEM(whole, BF),),
                    moved=10**6,
                )(ids, table, back)

    late = [lax.ppermute(back, "section", [(k, NS - 1)]) for k in range(NS - 1)]
    final = call(
        late_kernel,
        full,
        (SMEM, SMEM) + (VMEM,) * NS + (pl.ANY,),
        to=spec(pl.ANY),
        scratch=(pltpu.VMEM((SLOTS, BR, M), BF), pltpu.SemaphoreType.DMA((SLOTS,))),
        moved=10**6,
        aliases={6: 0},
    )(sec_ref, ids, *late, back, final)

    embedded = call(
        embed_kernel,
        jax.ShapeDtypeStruct((EV, M), BF),
        (VMEM,) * 4,
        flops=2 * EV * M * (2 * ROWS + M),
        moved=10**6,
    )(source.reshape(1, EV), near, kept, w_neighbour)
    return (final.reshape(1, BLOCKS * BR, M), embedded[None])


def solution(mesh):
    return jax.shard_map(
        on_device,
        mesh=mesh,
        in_specs=(
            P("shard", None),
            P("shard"),
            P("section", "shard", None, None),
            P("section", "shard"),
            P("section", "shard"),
            P("section", "shard"),
            P("section", "shard", None),
            P(),
            P(),
            P(),
            P(),
            P(),
            P(),
        ),
        out_specs=(P("section", "shard", None), P("section", "shard", None)),
        check_vma=False,
    )
```

```python
import functools

import jax
import jax.numpy as jnp
from jax import lax
from jax.experimental import pallas as pl
from jax.experimental.pallas import tpu as pltpu
from jax.sharding import PartitionSpec as P

BR = 8
NS = 4
LANES = 128
SLOTS = 64
ROWS = SLOTS * BR
EV = 256
BLOCKS = 256
M = 512
PUT = NS * BR
GET = PUT + NS
BF = jnp.bfloat16
F32 = jnp.float32
I32 = jnp.int32
VMEM = pltpu.VMEM
SMEM = pltpu.SMEM
HBM = pltpu.HBM
NT = (((1,), (1,)), ((), ()))


def spec(space=VMEM):
    return pl.BlockSpec(memory_space=space)


def call(body, outs, ins, to=None, scratch=(), flops=0, moved=0, aliases=None, mib=16):
    return pl.pallas_call(
        body,
        out_shape=outs,
        in_specs=[spec(s) for s in ins],
        out_specs=jax.tree.map(lambda _: spec(), outs) if to is None else to,
        scratch_shapes=list(scratch),
        input_output_aliases=aliases or {},
        compiler_params=pltpu.CompilerParams(vmem_limit_bytes=mib * 1024 * 1024),
        cost_estimate=pl.CostEstimate(flops=flops, bytes_accessed=moved, transcendentals=0),
    )


def wide(rows, at):
    return jnp.concatenate([rows[at : at + 1, :], rows[at + 1 : at + 2, :]], axis=1)


def message_rows(rows):
    source, target, when = wide(rows, 0), wide(rows, 2), wide(rows, 4)
    return (
        jnp.concatenate([source, target], axis=1),
        jnp.concatenate([target, source], axis=1),
        jnp.concatenate([when, when], axis=1),
    )


def as_column(row):
    n = row.shape[1]
    eye = lax.broadcasted_iota(I32, (n, n), 0) == lax.broadcasted_iota(I32, (n, n), 1)
    return jnp.sum(jnp.where(eye, row, jnp.zeros_like(row)), axis=1, keepdims=True)


def prep_kernel(sec_ref, w_in_ref, w_hid_ref, bias_ref, in_out, hid_out, bias_out):
    for g in range(3):
        column = pl.multiple_of(g * M + sec_ref[0] * LANES, LANES)
        for src, dst in ((w_in_ref, in_out), (w_hid_ref, hid_out), (bias_ref, bias_out)):
            dst[:, g * LANES : (g + 1) * LANES] = src[:, pl.ds(column, LANES)]


def events_kernel(sec_ref, ev_ref, pay_ref):
    sec = sec_ref[0]
    block = lax.broadcasted_iota(I32, (SLOTS, 2 * EV), 0) * BR
    lane = lax.broadcasted_iota(I32, (SLOTS, LANES), 1)
    pay = jnp.zeros((SLOTS, LANES), I32)
    for b in range(NS):
        rows = ev_ref[lax.rem(b + NS - sec, NS)]
        to, _, when = message_rows(rows)
        place = to - block
        for r in range(BR):
            latest = jnp.max(jnp.where(place == r, when, 0), axis=1, keepdims=True)
            pay = jnp.where(lane == b * BR + r, latest, pay)
        asked = as_column(rows[6:7, 0:SLOTS])
        pay = jnp.where(lane == PUT + b, jnp.where(asked < 0, BLOCKS, asked), pay)
        pay = jnp.where(lane == GET + b, jnp.where(asked < 0, BLOCKS + 1, asked), pay)
    pay_ref[...] = pay


def owner_kernel(got_ref, last_ref, table_ref, out_ref, rows_ref, table_out, ids_ref, sem):
    got = got_ref[...]
    flipped = jnp.transpose(
        jnp.concatenate([got.astype(F32), jnp.zeros((LANES - SLOTS, LANES), F32)], axis=0)
    ).astype(I32)
    rows_ref[...] = flipped[PUT : PUT + 2 * NS, :]
    scalars = pltpu.make_async_copy(rows_ref, ids_ref, sem)
    scalars.start()
    table_out[:BLOCKS] = table_ref[...]
    table_out[BLOCKS:] = jnp.zeros((8, BR, LANES), BF)
    cand = BLOCKS + NS * SLOTS
    lane = lax.broadcasted_iota(I32, (SLOTS, cand), 1)
    group = lax.broadcasted_iota(I32, (SLOTS, LANES), 1) // BR
    ids_row = jnp.concatenate(
        [lax.broadcasted_iota(I32, (1, BLOCKS), 1)]
        + [flipped[PUT + b : PUT + b + 1, 0:SLOTS] for b in range(NS)],
        axis=1,
    )
    match = jnp.concatenate(
        [
            ((got[:, GET + b : GET + b + 1] == ids_row) & (lane < BLOCKS + SLOTS * b)).astype(F32)
            for b in range(NS)
        ],
        axis=0,
    ).astype(BF)
    base = jnp.concatenate(
        [jnp.zeros((BLOCKS, (NS - 1) * BR), I32), last_ref[...], jnp.zeros((BLOCKS, LANES - NS * BR), I32)],
        axis=1,
    )
    times = jnp.concatenate(
        [base] + [jnp.where(group == b, got, 0) for b in range(NS - 1)] + [jnp.zeros((SLOTS, LANES), I32)],
        axis=0,
    )
    high = jnp.dot(match, (times >> 6).astype(F32).astype(BF), preferred_element_type=F32)
    low = jnp.dot(match, (times & 63).astype(F32).astype(BF), preferred_element_type=F32)
    stamp = high * 64.0 + low
    stamp = jnp.maximum(stamp, pltpu.roll(stamp, LANES - 2 * BR, 1))
    stamp = jnp.maximum(stamp, pltpu.roll(stamp, LANES - BR, 1)).astype(I32)
    total = jnp.zeros((SLOTS, LANES), I32)
    for b in range(NS):
        part = stamp[b * SLOTS : (b + 1) * SLOTS]
        part = pltpu.roll(part, b * BR, 1) if b else part
        total = jnp.where(group == b, part, total)
    packed = (total >> 6) + pltpu.roll(total & 63, PUT, 1)
    spread = jnp.broadcast_to(packed.astype(F32)[:, None, :], (SLOTS, BR, LANES))
    out_ref[:, :, LANES : 2 * LANES] = spread.astype(BF)
    scalars.wait()
    for j in range(SLOTS):
        out_ref[j, :, 0:LANES] = table_out[ids_ref[NS, j]]


def swap_kernel(b, ids_ref, table_ref, back_ref, out_ref, table_out):
    table_out[...] = table_ref[...]
    for j in range(SLOTS):
        table_out[ids_ref[b, j]] = back_ref[j]
    for j in range(SLOTS):
        out_ref[j] = table_out[ids_ref[NS + b + 1, j]]


def cosine(x):
    turns = jnp.round(x * 0.15915494309189535)
    x = x - turns * 6.28125
    x = x - turns * 0.0019340515136718750
    x = x - turns * 1.255665914e-06
    y = x * x
    total = jnp.full_like(y, -1.1470745597729725e-11)
    for c in (
        2.0876756987868099e-09,
        -2.7557319223985893e-07,
        2.4801587301587302e-05,
        -1.3888888888888889e-03,
        4.1666666666666667e-02,
        -0.5,
        1.0,
    ):
        total = total * y + c
    return total


def code_kernel(b, sec_ref, ev_ref, stamp_ref, rate_ref, phase_ref, out_ref, pair_ref, share_ref):
    rows = ev_ref[lax.rem(b + NS - sec_ref[0], NS)]
    to, other, when = message_rows(rows)
    lane = lax.broadcasted_iota(I32, (ROWS, LANES), 1)
    sub = lax.broadcasted_iota(I32, (ROWS, LANES), 0) & (BR - 1)
    stamps = stamp_ref[:, LANES : 2 * LANES].astype(F32)
    scale = jnp.where(lane == b * BR + sub, 64.0, jnp.where(lane == PUT + b * BR + sub, 1.0, 0.0))
    state_time = jnp.sum(stamps * scale, axis=1, keepdims=True)
    slot = lax.broadcasted_iota(I32, (ROWS, 2 * EV), 0)
    hit = slot == to
    before = jnp.sum(jnp.where(hit, state_time, 0.0), axis=0, keepdims=True)
    delta = when.astype(F32) - before
    code = cosine(as_column(rate_ref[...]) * delta + as_column(phase_ref[...]))
    high = code.astype(BF)
    low = (code - high.astype(F32)).astype(BF)
    hits = hit.astype(F32)
    counts = jnp.sum(hits, axis=1, keepdims=True)
    hits = hits.astype(BF)
    total = lax.dot_general(hits, high, NT, preferred_element_type=F32)
    total = total + lax.dot_general(hits, low, NT, preferred_element_type=F32)
    out_ref[...] = (total / jnp.maximum(counts, 1.0)).astype(BF)
    share_ref[...] = jnp.where(counts > 0.0, 1.0 / jnp.maximum(counts, 1.0), 0.0)
    partner = (slot == other).astype(F32).astype(BF)
    pair_ref[...] = lax.dot_general(hits, partner, NT, preferred_element_type=F32).astype(BF)


def cell_kernel(
    b,
    sec_ref,
    own_ref,
    one_ref,
    two_ref,
    three_ref,
    pair_ref,
    code_ref,
    share_ref,
    w_in_ref,
    w_hid_ref,
    bias_ref,
    *refs,
):
    new_ref, kept_ref, all_ref, sem = refs[-4:]
    sec = sec_ref[0]
    for k, part in enumerate((own_ref, one_ref, two_ref, three_ref)):
        at = pl.multiple_of(lax.rem(sec + k, NS) * LANES, LANES)
        all_ref[:, pl.ds(at, LANES)] = part[...]
    keep = pltpu.make_async_copy(all_ref.at[:, 0:M], kept_ref, sem)

    @pl.when(sec == b)
    def _():
        keep.start()

    share = share_ref[...]
    states = all_ref[:, 0:M]
    trail = jnp.dot(pair_ref[...], states, preferred_element_type=F32) * share
    all_ref[:, M : 2 * M] = trail.astype(BF)
    all_ref[:, 2 * M :] = code_ref[...]
    carried = jnp.dot(states, w_hid_ref[...], preferred_element_type=F32)
    into = jnp.dot(all_ref[...], w_in_ref[...], preferred_element_type=F32) + bias_ref[...]
    gates = 0.5 + 0.5 * jnp.tanh(0.5 * (into[:, : 2 * LANES] + carried[:, : 2 * LANES]))
    reset, update = gates[:, :LANES], gates[:, LANES:]
    candidate = jnp.tanh(into[:, 2 * LANES :] + reset * carried[:, 2 * LANES :])
    old = own_ref[...].astype(F32)
    new = (1.0 - update) * candidate + update * old
    new_ref[...] = jnp.where(share > 0.0, new, old).astype(BF)

    @pl.when(sec == b)
    def _():
        keep.wait()


def early_kernel(sec_ref, ids_ref, mem_ref, own_ref, one_ref, two_ref, three_ref, out_ref, full_ref, sem):
    sec = sec_ref[0]
    fill = pltpu.make_async_copy(mem_ref, full_ref.at[pl.ds(0, BLOCKS)], sem)
    fill.start()
    fill.wait()
    for b in range(NS - 1):

        @pl.when(sec >= b)
        def _():
            for k, part in enumerate((own_ref, one_ref, two_ref, three_ref)):
                to = pl.multiple_of(lax.rem(sec + k, NS) * LANES, LANES)
                for j in range(SLOTS):
                    full_ref[ids_ref[b, j], :, pl.ds(to, LANES)] = part[b, j]

    drain = pltpu.make_async_copy(full_ref.at[pl.ds(0, BLOCKS)], out_ref, sem)
    drain.start()
    drain.wait()


def late_kernel(sec_ref, ids_ref, zero_ref, one_ref, two_ref, own_ref, early_ref, out_ref, full_ref, sems):
    @pl.when(sec_ref[0] == NS - 1)
    def _():
        for k, part in enumerate((zero_ref, one_ref, two_ref, own_ref)):
            full_ref[:, :, k * LANES : (k + 1) * LANES] = part[...]

        def place(j):
            at = ids_ref[NS - 1, j]
            return at, pltpu.make_async_copy(
                full_ref.at[j], out_ref.at[jnp.minimum(at, BLOCKS - 1)], sems.at[j]
            )

        for j in range(SLOTS):
            at, copy = place(j)

            @pl.when(at < BLOCKS)
            def _():
                copy.start()

        for j in range(SLOTS):
            at, copy = place(j)

            @pl.when(at < BLOCKS)
            def _():
                copy.wait()


def embed_kernel(source_ref, near_ref, kept_ref, weight_ref, out_ref):
    slot = lax.broadcasted_iota(I32, (EV, ROWS), 1)
    block = slot >> 3
    picks = jnp.zeros((EV, ROWS), F32)
    for k in range(near_ref.shape[0]):
        picks = picks + jnp.where(block == as_column(near_ref[k : k + 1, :]), 1.0 / BR, 0.0)
    states = kept_ref[...]
    near = jnp.dot(picks.astype(BF), states, preferred_element_type=F32).astype(BF)
    mixed = jnp.dot(near, weight_ref[...], preferred_element_type=F32)
    own = (slot == as_column(source_ref[...])).astype(F32).astype(BF)
    out_ref[...] = (jnp.dot(own, states, preferred_element_type=F32) + mixed).astype(BF)


def from_sections(array):
    return [array] + [
        lax.ppermute(array, "section", [(i, (i - k) % NS) for i in range(NS)]) for k in range(1, NS)
    ]


def exchange(array):
    return lax.all_to_all(array, "shard", split_axis=0, concat_axis=0, tiled=True)


def on_device(
    memory,
    last_time,
    requests,
    event_source,
    event_target,
    event_time,
    neighbour_blocks,
    time_rates,
    time_phase,
    w_input,
    w_hidden,
    bias_input,
    w_neighbour,
):
    sec = lax.axis_index("section")
    sec_ref = sec.astype(I32).reshape(1)
    source = event_source[0]
    ints = jnp.concatenate(
        [
            source,
            event_target[0],
            event_time[0],
            requests.reshape(SLOTS),
            jnp.zeros((8 * LANES - 3 * EV - SLOTS,), I32),
        ]
    ).reshape(8, LANES)
    parts = from_sections(ints)
    table = lax.dynamic_slice_in_dim(memory, sec * LANES, LANES, axis=1)
    last = last_time.reshape(BLOCKS, BR)
    bias_row = bias_input.reshape(1, -1)
    parts, table, last, bias_row = lax.optimization_barrier((parts, table, last, bias_row))
    events = jnp.stack(parts)
    pay = call(
        events_kernel, jax.ShapeDtypeStruct((SLOTS, LANES), I32), (SMEM, VMEM), moved=10**6
    )(sec_ref, events)
    ids = exchange(pay.reshape(SLOTS, 1, LANES)).reshape(SLOTS, LANES)
    picked, ids, table = call(
        owner_kernel,
        (
            jax.ShapeDtypeStruct((SLOTS, BR, 2 * LANES), BF),
            jax.ShapeDtypeStruct((2 * NS, LANES), I32),
            jax.ShapeDtypeStruct((BLOCKS + 8, BR, LANES), BF),
        ),
        (VMEM, VMEM, VMEM),
        scratch=(pltpu.SMEM((2 * NS, LANES), I32), pltpu.SemaphoreType.DMA),
        moved=10**6,
    )(ids, last, table.reshape(BLOCKS, BR, LANES))
    stamps = kept = None
    backs = []
    for b in range(NS):
        pulled = exchange(picked).reshape(ROWS, -1)
        if b == 0:
            stamps = pulled
            pulled = pulled[:, :LANES]
            pulled, later = lax.optimization_barrier((pulled, sec_ref))
            w_in, w_hid, bias = call(
                prep_kernel,
                (
                    jax.ShapeDtypeStruct((w_input.shape[0], 3 * LANES), BF),
                    jax.ShapeDtypeStruct((M, 3 * LANES), BF),
                    jax.ShapeDtypeStruct((1, 3 * LANES), F32),
                ),
                (SMEM, VMEM, VMEM, VMEM),
                moved=3 * 10**6,
            )(later, w_input, w_hidden, bias_row)
        if b == NS - 1:
            early = from_sections(jnp.stack(backs))
            pulled, early[1] = lax.optimization_barrier((pulled, early[1]))
        parts = from_sections(pulled)
        if b == NS - 1:
            full = jax.ShapeDtypeStruct((BLOCKS, BR, M), BF)
            final = call(
                early_kernel,
                full,
                (SMEM, SMEM, pl.ANY) + (VMEM,) * NS,
                to=spec(pl.ANY),
                scratch=(pltpu.VMEM((BLOCKS + 8, BR, M), BF), pltpu.SemaphoreType.DMA),
                moved=8 * 10**6,
            )(sec_ref, ids, memory.reshape(BLOCKS, BR, M), *early)
            parts, final = lax.optimization_barrier((parts, final))
        code, pairs, share = call(
            functools.partial(code_kernel, b),
            (
                jax.ShapeDtypeStruct((ROWS, LANES), BF),
                jax.ShapeDtypeStruct((ROWS, ROWS), BF),
                jax.ShapeDtypeStruct((ROWS, 1), F32),
            ),
            (SMEM, VMEM, VMEM, VMEM, VMEM),
            flops=2 * ROWS**3,
            moved=10**6,
        )(sec_ref, events, stamps, time_rates.reshape(1, LANES), time_phase.reshape(1, LANES))
        updated, kept = call(
            functools.partial(cell_kernel, b),
            (jax.ShapeDtypeStruct((ROWS, LANES), BF), jax.ShapeDtypeStruct((ROWS, M), BF)),
            (SMEM,) + (VMEM,) * 10 + ((pl.ANY,) if b else ()),
            to=(spec(), spec(pl.ANY)),
            scratch=(pltpu.VMEM((ROWS, 2 * M + LANES), BF), pltpu.SemaphoreType.DMA),
            flops=2 * ROWS * M * (M + 9 * LANES),
            moved=4 * 10**6,
            aliases={11: 1} if b else None,
        )(sec_ref, *parts, pairs, code, share, w_in, w_hid, bias, *([kept] if b else []))
        updated = updated.reshape(SLOTS, BR, LANES)
        if b == NS - 1:
            updated, near, source = lax.optimization_barrier(
                (updated, neighbour_blocks[0].T, source)
            )
        back = exchange(updated)
        if b < NS - 1:
            backs.append(back)
            block = jax.ShapeDtypeStruct((SLOTS, BR, LANES), BF)
            whole = (BLOCKS + 8, BR, LANES)
            if b < NS - 2:
                picked, table = call(
                    functools.partial(swap_kernel, b),
                    (block, jax.ShapeDtypeStruct(whole, BF)),
                    (SMEM, VMEM, VMEM),
                    moved=10**6,
                )(ids, table, back)
            else:
                picked = call(
                    functools.partial(swap_kernel, b),
                    block,
                    (SMEM, VMEM, VMEM),
                    scratch=(pltpu.VMEM(whole, BF),),
                    moved=10**6,
                )(ids, table, back)

    late = [lax.ppermute(back, "section", [(k, NS - 1)]) for k in range(NS - 1)]
    final = call(
        late_kernel,
        full,
        (SMEM, SMEM) + (VMEM,) * NS + (pl.ANY,),
        to=spec(pl.ANY),
        scratch=(pltpu.VMEM((SLOTS, BR, M), BF), pltpu.SemaphoreType.DMA((SLOTS,))),
        moved=10**6,
        aliases={6: 0},
    )(sec_ref, ids, *late, back, final)

    embedded = call(
        embed_kernel,
        jax.ShapeDtypeStruct((EV, M), BF),
        (VMEM,) * 4,
        flops=2 * EV * M * (2 * ROWS + M),
        moved=10**6,
    )(source.reshape(1, EV), near, kept, w_neighbour)
    return (final.reshape(1, BLOCKS * BR, M), embedded[None])


def solution(mesh):
    return jax.shard_map(
        on_device,
        mesh=mesh,
        in_specs=(
            P("shard", None),
            P("shard"),
            P("section", "shard", None, None),
            P("section", "shard"),
            P("section", "shard"),
            P("section", "shard"),
            P("section", "shard", None),
            P(),
            P(),
            P(),
            P(),
            P(),
            P(),
        ),
        out_specs=(P("section", "shard", None), P("section", "shard", None)),
        check_vma=False,
    )
```

```python
import functools

import jax
import jax.numpy as jnp
from jax import lax
from jax.experimental import pallas as pl
from jax.experimental.pallas import tpu as pltpu
from jax.sharding import PartitionSpec as P

BR = 8
NS = 4
LANES = 128
SLOTS = 64
ROWS = SLOTS * BR
EV = 256
BLOCKS = 256
M = 512
PUT = NS * BR
GET = PUT + NS
BF = jnp.bfloat16
F32 = jnp.float32
I32 = jnp.int32
VMEM = pltpu.VMEM
SMEM = pltpu.SMEM
HBM = pltpu.HBM
NT = (((1,), (1,)), ((), ()))


def spec(space=VMEM):
    return pl.BlockSpec(memory_space=space)


def call(body, outs, ins, to=None, scratch=(), flops=0, moved=0, aliases=None, mib=16):
    return pl.pallas_call(
        body,
        out_shape=outs,
        in_specs=[spec(s) for s in ins],
        out_specs=jax.tree.map(lambda _: spec(), outs) if to is None else to,
        scratch_shapes=list(scratch),
        input_output_aliases=aliases or {},
        compiler_params=pltpu.CompilerParams(vmem_limit_bytes=mib * 1024 * 1024),
        cost_estimate=pl.CostEstimate(flops=flops, bytes_accessed=moved, transcendentals=0),
    )


def wide(rows, at):
    return jnp.concatenate([rows[at : at + 1, :], rows[at + 1 : at + 2, :]], axis=1)


def message_rows(rows):
    source, target, when = wide(rows, 0), wide(rows, 2), wide(rows, 4)
    return (
        jnp.concatenate([source, target], axis=1),
        jnp.concatenate([target, source], axis=1),
        jnp.concatenate([when, when], axis=1),
    )


def as_column(row):
    n = row.shape[1]
    eye = lax.broadcasted_iota(I32, (n, n), 0) == lax.broadcasted_iota(I32, (n, n), 1)
    return jnp.sum(jnp.where(eye, row, jnp.zeros_like(row)), axis=1, keepdims=True)


def prep_kernel(sec_ref, w_in_ref, w_hid_ref, bias_ref, both_out, hid_out, code_out, bias_out):
    def quarter(g):
        return pl.ds(pl.multiple_of(g * M + sec_ref[0] * LANES, LANES), LANES)

    for g in range(3):
        to = slice(g * LANES, (g + 1) * LANES)
        both_out[:, to] = w_in_ref[0 : 2 * M, quarter(g)]
        code_out[:, to] = w_in_ref[2 * M :, quarter(g)]
        bias_out[:, to] = bias_ref[:, quarter(g)]
    for g in range(2):
        hid_out[:, g * LANES : (g + 1) * LANES] = w_hid_ref[:, quarter(g)]
    both_out[0:M, 3 * LANES :] = w_hid_ref[:, quarter(2)]
    both_out[M:, 3 * LANES :] = jnp.zeros((M, LANES), BF)


def events_kernel(sec_ref, ev_ref, pay_ref):
    sec = sec_ref[0]
    block = lax.broadcasted_iota(I32, (SLOTS, 2 * EV), 0) * BR
    lane = lax.broadcasted_iota(I32, (SLOTS, LANES), 1)
    pay = jnp.zeros((SLOTS, LANES), I32)
    for b in range(NS):
        rows = ev_ref[lax.rem(b + NS - sec, NS)]
        to, _, when = message_rows(rows)
        place = to - block
        for r in range(BR):
            latest = jnp.max(jnp.where(place == r, when, 0), axis=1, keepdims=True)
            pay = jnp.where(lane == b * BR + r, latest, pay)
        asked = as_column(rows[6:7, 0:SLOTS])
        pay = jnp.where(lane == PUT + b, jnp.where(asked < 0, BLOCKS, asked), pay)
        pay = jnp.where(lane == GET + b, jnp.where(asked < 0, BLOCKS + 1, asked), pay)
    pay_ref[...] = pay


def owner_kernel(got_ref, last_ref, table_ref, out_ref, rows_ref, table_out, ids_ref, sem):
    got = got_ref[...]
    flipped = jnp.transpose(
        jnp.concatenate([got.astype(F32), jnp.zeros((LANES - SLOTS, LANES), F32)], axis=0)
    ).astype(I32)
    rows_ref[...] = flipped[PUT : PUT + 2 * NS, :]
    scalars = pltpu.make_async_copy(rows_ref, ids_ref, sem)
    scalars.start()
    table_out[:BLOCKS] = table_ref[...]
    table_out[BLOCKS:] = jnp.zeros((8, BR, LANES), BF)
    cand = BLOCKS + NS * SLOTS
    lane = lax.broadcasted_iota(I32, (SLOTS, cand), 1)
    group = lax.broadcasted_iota(I32, (SLOTS, LANES), 1) // BR
    ids_row = jnp.concatenate(
        [lax.broadcasted_iota(I32, (1, BLOCKS), 1)]
        + [flipped[PUT + b : PUT + b + 1, 0:SLOTS] for b in range(NS)],
        axis=1,
    )
    match = jnp.concatenate(
        [
            ((got[:, GET + b : GET + b + 1] == ids_row) & (lane < BLOCKS + SLOTS * b)).astype(F32)
            for b in range(NS)
        ],
        axis=0,
    ).astype(BF)
    base = jnp.concatenate(
        [jnp.zeros((BLOCKS, (NS - 1) * BR), I32), last_ref[...], jnp.zeros((BLOCKS, LANES - NS * BR), I32)],
        axis=1,
    )
    times = jnp.concatenate(
        [base] + [jnp.where(group == b, got, 0) for b in range(NS - 1)] + [jnp.zeros((SLOTS, LANES), I32)],
        axis=0,
    )
    high = jnp.dot(match, (times >> 6).astype(F32).astype(BF), preferred_element_type=F32)
    low = jnp.dot(match, (times & 63).astype(F32).astype(BF), preferred_element_type=F32)
    stamp = high * 64.0 + low
    stamp = jnp.maximum(stamp, pltpu.roll(stamp, LANES - 2 * BR, 1))
    stamp = jnp.maximum(stamp, pltpu.roll(stamp, LANES - BR, 1)).astype(I32)
    total = jnp.zeros((SLOTS, LANES), I32)
    for b in range(NS):
        part = stamp[b * SLOTS : (b + 1) * SLOTS]
        part = pltpu.roll(part, b * BR, 1) if b else part
        total = jnp.where(group == b, part, total)
    packed = (total >> 6) + pltpu.roll(total & 63, PUT, 1)
    spread = jnp.broadcast_to(packed.astype(F32)[:, None, :], (SLOTS, BR, LANES))
    out_ref[:, :, LANES : 2 * LANES] = spread.astype(BF)
    scalars.wait()
    for j in range(SLOTS):
        out_ref[j, :, 0:LANES] = table_out[ids_ref[NS, j]]


def swap_kernel(b, ids_ref, table_ref, back_ref, out_ref, table_out):
    table_out[...] = table_ref[...]
    for j in range(SLOTS):
        table_out[ids_ref[b, j]] = back_ref[j]
    for j in range(SLOTS):
        out_ref[j] = table_out[ids_ref[NS + b + 1, j]]


def cosine(x):
    turns = jnp.round(x * 0.15915494309189535)
    x = x - turns * 6.28125
    x = x - turns * 0.0019340515136718750
    x = x - turns * 1.255665914e-06
    y = x * x
    total = jnp.full_like(y, -1.1470745597729725e-11)
    for c in (
        2.0876756987868099e-09,
        -2.7557319223985893e-07,
        2.4801587301587302e-05,
        -1.3888888888888889e-03,
        4.1666666666666667e-02,
        -0.5,
        1.0,
    ):
        total = total * y + c
    return total


def code_kernel(
    b,
    sec_ref,
    ev_ref,
    stamp_ref,
    rate_ref,
    phase_ref,
    w_code_ref,
    bias_ref,
    out_ref,
    pair_ref,
    share_ref,
):
    rows = ev_ref[lax.rem(b + NS - sec_ref[0], NS)]
    to, other, when = message_rows(rows)
    lane = lax.broadcasted_iota(I32, (ROWS, LANES), 1)
    sub = lax.broadcasted_iota(I32, (ROWS, LANES), 0) & (BR - 1)
    stamps = stamp_ref[:, LANES : 2 * LANES].astype(F32)
    scale = jnp.where(lane == b * BR + sub, 64.0, jnp.where(lane == PUT + b * BR + sub, 1.0, 0.0))
    state_time = jnp.sum(stamps * scale, axis=1, keepdims=True)
    slot = lax.broadcasted_iota(I32, (ROWS, 2 * EV), 0)
    hit = slot == to
    before = jnp.sum(jnp.where(hit, state_time, 0.0), axis=0, keepdims=True)
    delta = when.astype(F32) - before
    code = cosine(as_column(rate_ref[...]) * delta + as_column(phase_ref[...]))
    high = code.astype(BF)
    low = (code - high.astype(F32)).astype(BF)
    hits = hit.astype(F32)
    counts = jnp.sum(hits, axis=1, keepdims=True)
    hits = hits.astype(BF)
    total = lax.dot_general(hits, high, NT, preferred_element_type=F32)
    total = total + lax.dot_general(hits, low, NT, preferred_element_type=F32)
    mean = (total / jnp.maximum(counts, 1.0)).astype(BF)
    out_ref[...] = jnp.dot(mean, w_code_ref[...], preferred_element_type=F32) + bias_ref[...]
    share_ref[...] = jnp.where(counts > 0.0, 1.0 / jnp.maximum(counts, 1.0), 0.0)
    partner = (slot == other).astype(F32).astype(BF)
    pair_ref[...] = lax.dot_general(hits, partner, NT, preferred_element_type=F32).astype(BF)


def cell_kernel(
    b,
    sec_ref,
    own_ref,
    one_ref,
    two_ref,
    three_ref,
    pair_ref,
    code_ref,
    share_ref,
    w_both_ref,
    w_hid_ref,
    *refs,
):
    new_ref, kept_ref, all_ref, sem = refs[-4:]
    sec = sec_ref[0]
    for k, part in enumerate((own_ref, one_ref, two_ref, three_ref)):
        at = pl.multiple_of(lax.rem(sec + k, NS) * LANES, LANES)
        all_ref[:, pl.ds(at, LANES)] = part[...]
    keep = pltpu.make_async_copy(all_ref.at[:, 0:M], kept_ref, sem)

    @pl.when(sec == b)
    def _():
        keep.start()

    share = share_ref[...]
    states = all_ref[:, 0:M]
    trail = jnp.dot(pair_ref[...], states, preferred_element_type=F32) * share
    all_ref[:, M:] = trail.astype(BF)
    both = jnp.dot(all_ref[...], w_both_ref[...], preferred_element_type=F32)
    carried = jnp.dot(states, w_hid_ref[...], preferred_element_type=F32)
    given = code_ref[...]
    gates = both[:, : 2 * LANES] + carried + given[:, : 2 * LANES]
    gates = 0.5 + 0.5 * jnp.tanh(0.5 * gates)
    reset, update = gates[:, :LANES], gates[:, LANES:]
    candidate = both[:, 2 * LANES : 3 * LANES] + given[:, 2 * LANES :]
    candidate = jnp.tanh(candidate + reset * both[:, 3 * LANES :])
    old = own_ref[...].astype(F32)
    new = (1.0 - update) * candidate + update * old
    new_ref[...] = jnp.where(share > 0.0, new, old).astype(BF)

    @pl.when(sec == b)
    def _():
        keep.wait()


def early_kernel(sec_ref, ids_ref, mem_ref, own_ref, one_ref, two_ref, three_ref, out_ref, full_ref, sem):
    sec = sec_ref[0]
    fill = pltpu.make_async_copy(mem_ref, full_ref.at[pl.ds(0, BLOCKS)], sem)
    fill.start()
    fill.wait()
    for b in range(NS - 1):

        @pl.when(sec >= b)
        def _():
            for k, part in enumerate((own_ref, one_ref, two_ref, three_ref)):
                to = pl.multiple_of(lax.rem(sec + k, NS) * LANES, LANES)
                for j in range(SLOTS):
                    full_ref[ids_ref[b, j], :, pl.ds(to, LANES)] = part[b, j]

    drain = pltpu.make_async_copy(full_ref.at[pl.ds(0, BLOCKS)], out_ref, sem)
    drain.start()
    drain.wait()


def late_kernel(sec_ref, ids_ref, zero_ref, one_ref, two_ref, own_ref, early_ref, out_ref, full_ref, sems):
    @pl.when(sec_ref[0] == NS - 1)
    def _():
        for k, part in enumerate((zero_ref, one_ref, two_ref, own_ref)):
            full_ref[:, :, k * LANES : (k + 1) * LANES] = part[...]

        def place(j):
            at = ids_ref[NS - 1, j]
            return at, pltpu.make_async_copy(
                full_ref.at[j], out_ref.at[jnp.minimum(at, BLOCKS - 1)], sems.at[j]
            )

        for j in range(SLOTS):
            at, copy = place(j)

            @pl.when(at < BLOCKS)
            def _():
                copy.start()

        for j in range(SLOTS):
            at, copy = place(j)

            @pl.when(at < BLOCKS)
            def _():
                copy.wait()


def embed_kernel(source_ref, near_ref, kept_ref, weight_ref, out_ref):
    slot = lax.broadcasted_iota(I32, (EV, ROWS), 1)
    block = slot >> 3
    picks = jnp.zeros((EV, ROWS), F32)
    for k in range(near_ref.shape[0]):
        picks = picks + jnp.where(block == as_column(near_ref[k : k + 1, :]), 1.0 / BR, 0.0)
    states = kept_ref[...]
    near = jnp.dot(picks.astype(BF), states, preferred_element_type=F32).astype(BF)
    mixed = jnp.dot(near, weight_ref[...], preferred_element_type=F32)
    own = (slot == as_column(source_ref[...])).astype(F32).astype(BF)
    out_ref[...] = (jnp.dot(own, states, preferred_element_type=F32) + mixed).astype(BF)


def from_sections(array):
    return [array] + [
        lax.ppermute(array, "section", [(i, (i - k) % NS) for i in range(NS)]) for k in range(1, NS)
    ]


def exchange(array):
    return lax.all_to_all(array, "shard", split_axis=0, concat_axis=0, tiled=True)


def on_device(
    memory,
    last_time,
    requests,
    event_source,
    event_target,
    event_time,
    neighbour_blocks,
    time_rates,
    time_phase,
    w_input,
    w_hidden,
    bias_input,
    w_neighbour,
):
    sec = lax.axis_index("section")
    sec_ref = sec.astype(I32).reshape(1)
    source = event_source[0]
    ints = jnp.concatenate(
        [
            source,
            event_target[0],
            event_time[0],
            requests.reshape(SLOTS),
            jnp.zeros((8 * LANES - 3 * EV - SLOTS,), I32),
        ]
    ).reshape(8, LANES)
    parts = from_sections(ints)
    table = lax.dynamic_slice_in_dim(memory, sec * LANES, LANES, axis=1)
    last = last_time.reshape(BLOCKS, BR)
    bias_row = bias_input.reshape(1, -1)
    parts, table, last, bias_row = lax.optimization_barrier((parts, table, last, bias_row))
    events = jnp.stack(parts)
    pay = call(
        events_kernel, jax.ShapeDtypeStruct((SLOTS, LANES), I32), (SMEM, VMEM), moved=10**6
    )(sec_ref, events)
    ids = exchange(pay.reshape(SLOTS, 1, LANES)).reshape(SLOTS, LANES)
    picked, ids, table = call(
        owner_kernel,
        (
            jax.ShapeDtypeStruct((SLOTS, BR, 2 * LANES), BF),
            jax.ShapeDtypeStruct((2 * NS, LANES), I32),
            jax.ShapeDtypeStruct((BLOCKS + 8, BR, LANES), BF),
        ),
        (VMEM, VMEM, VMEM),
        scratch=(pltpu.SMEM((2 * NS, LANES), I32), pltpu.SemaphoreType.DMA),
        moved=10**6,
    )(ids, last, table.reshape(BLOCKS, BR, LANES))
    stamps = kept = None
    backs = []
    for b in range(NS):
        pulled = exchange(picked).reshape(ROWS, -1)
        if b == 0:
            stamps = pulled
            pulled = pulled[:, :LANES]
            pulled, later = lax.optimization_barrier((pulled, sec_ref))
            w_both, w_hid, w_code, bias = call(
                prep_kernel,
                (
                    jax.ShapeDtypeStruct((2 * M, 4 * LANES), BF),
                    jax.ShapeDtypeStruct((M, 2 * LANES), BF),
                    jax.ShapeDtypeStruct((LANES, 3 * LANES), BF),
                    jax.ShapeDtypeStruct((1, 3 * LANES), F32),
                ),
                (SMEM, VMEM, VMEM, VMEM),
                moved=3 * 10**6,
            )(later, w_input, w_hidden, bias_row)
        if b == NS - 1:
            early = from_sections(jnp.stack(backs))
            pulled, early[1] = lax.optimization_barrier((pulled, early[1]))
        parts = from_sections(pulled)
        if b == NS - 1:
            full = jax.ShapeDtypeStruct((BLOCKS, BR, M), BF)
            final = call(
                early_kernel,
                full,
                (SMEM, SMEM, pl.ANY) + (VMEM,) * NS,
                to=spec(pl.ANY),
                scratch=(pltpu.VMEM((BLOCKS + 8, BR, M), BF), pltpu.SemaphoreType.DMA),
                moved=8 * 10**6,
            )(sec_ref, ids, memory.reshape(BLOCKS, BR, M), *early)
            parts, final = lax.optimization_barrier((parts, final))
        code, pairs, share = call(
            functools.partial(code_kernel, b),
            (
                jax.ShapeDtypeStruct((ROWS, 3 * LANES), F32),
                jax.ShapeDtypeStruct((ROWS, ROWS), BF),
                jax.ShapeDtypeStruct((ROWS, 1), F32),
            ),
            (SMEM,) + (VMEM,) * 6,
            flops=2 * ROWS**3,
            moved=10**6,
        )(
            sec_ref,
            events,
            stamps,
            time_rates.reshape(1, LANES),
            time_phase.reshape(1, LANES),
            w_code,
            bias,
        )
        updated, kept = call(
            functools.partial(cell_kernel, b),
            (jax.ShapeDtypeStruct((ROWS, LANES), BF), jax.ShapeDtypeStruct((ROWS, M), BF)),
            (SMEM,) + (VMEM,) * 9 + ((pl.ANY,) if b else ()),
            to=(spec(), spec(pl.ANY)),
            scratch=(pltpu.VMEM((ROWS, 2 * M), BF), pltpu.SemaphoreType.DMA),
            flops=2 * ROWS * M * (M + 9 * LANES),
            moved=4 * 10**6,
            aliases={10: 1} if b else None,
        )(sec_ref, *parts, pairs, code, share, w_both, w_hid, *([kept] if b else []))
        updated = updated.reshape(SLOTS, BR, LANES)
        if b == NS - 1:
            updated, near, source = lax.optimization_barrier(
                (updated, neighbour_blocks[0].T, source)
            )
        back = exchange(updated)
        if b < NS - 1:
            backs.append(back)
            block = jax.ShapeDtypeStruct((SLOTS, BR, LANES), BF)
            whole = (BLOCKS + 8, BR, LANES)
            if b < NS - 2:
                picked, table = call(
                    functools.partial(swap_kernel, b),
                    (block, jax.ShapeDtypeStruct(whole, BF)),
                    (SMEM, VMEM, VMEM),
                    moved=10**6,
                )(ids, table, back)
            else:
                picked = call(
                    functools.partial(swap_kernel, b),
                    block,
                    (SMEM, VMEM, VMEM),
                    scratch=(pltpu.VMEM(whole, BF),),
                    moved=10**6,
                )(ids, table, back)

    late = [lax.ppermute(back, "section", [(k, NS - 1)]) for k in range(NS - 1)]
    final = call(
        late_kernel,
        full,
        (SMEM, SMEM) + (VMEM,) * NS + (pl.ANY,),
        to=spec(pl.ANY),
        scratch=(pltpu.VMEM((SLOTS, BR, M), BF), pltpu.SemaphoreType.DMA((SLOTS,))),
        moved=10**6,
        aliases={6: 0},
    )(sec_ref, ids, *late, back, final)

    embedded = call(
        embed_kernel,
        jax.ShapeDtypeStruct((EV, M), BF),
        (VMEM,) * 4,
        flops=2 * EV * M * (2 * ROWS + M),
        moved=10**6,
    )(source.reshape(1, EV), near, kept, w_neighbour)
    return (final.reshape(1, BLOCKS * BR, M), embedded[None])


def solution(mesh):
    return jax.shard_map(
        on_device,
        mesh=mesh,
        in_specs=(
            P("shard", None),
            P("shard"),
            P("section", "shard", None, None),
            P("section", "shard"),
            P("section", "shard"),
            P("section", "shard"),
            P("section", "shard", None),
            P(),
            P(),
            P(),
            P(),
            P(),
            P(),
        ),
        out_specs=(P("section", "shard", None), P("section", "shard", None)),
        check_vma=False,
    )
```

```python
import functools

import jax
import jax.numpy as jnp
from jax import lax
from jax.experimental import pallas as pl
from jax.experimental.pallas import tpu as pltpu
from jax.sharding import PartitionSpec as P

BR = 8
NS = 4
LANES = 128
SLOTS = 64
ROWS = SLOTS * BR
EV = 256
BLOCKS = 256
M = 512
PUT = NS * BR
GET = PUT + NS
BF = jnp.bfloat16
F32 = jnp.float32
I32 = jnp.int32
VMEM = pltpu.VMEM
SMEM = pltpu.SMEM
HBM = pltpu.HBM
NT = (((1,), (1,)), ((), ()))


def spec(space=VMEM):
    return pl.BlockSpec(memory_space=space)


def call(body, outs, ins, to=None, scratch=(), flops=0, moved=0, aliases=None, mib=16):
    return pl.pallas_call(
        body,
        out_shape=outs,
        in_specs=[spec(s) for s in ins],
        out_specs=jax.tree.map(lambda _: spec(), outs) if to is None else to,
        scratch_shapes=list(scratch),
        input_output_aliases=aliases or {},
        compiler_params=pltpu.CompilerParams(vmem_limit_bytes=mib * 1024 * 1024),
        cost_estimate=pl.CostEstimate(flops=flops, bytes_accessed=moved, transcendentals=0),
    )


def wide(rows, at):
    return jnp.concatenate([rows[at : at + 1, :], rows[at + 1 : at + 2, :]], axis=1)


def message_rows(rows):
    source, target, when = wide(rows, 0), wide(rows, 2), wide(rows, 4)
    return (
        jnp.concatenate([source, target], axis=1),
        jnp.concatenate([target, source], axis=1),
        jnp.concatenate([when, when], axis=1),
    )


def as_column(row):
    n = row.shape[1]
    eye = lax.broadcasted_iota(I32, (n, n), 0) == lax.broadcasted_iota(I32, (n, n), 1)
    return jnp.sum(jnp.where(eye, row, jnp.zeros_like(row)), axis=1, keepdims=True)


def prep_kernel(sec_ref, w_in_ref, w_hid_ref, bias_ref, both_out, hid_out, code_out, bias_out):
    def quarter(g):
        return pl.ds(pl.multiple_of(g * M + sec_ref[0] * LANES, LANES), LANES)

    for g in range(3):
        to = slice(g * LANES, (g + 1) * LANES)
        both_out[:, to] = w_in_ref[0 : 2 * M, quarter(g)]
        code_out[:, to] = w_in_ref[2 * M :, quarter(g)]
        bias_out[:, to] = bias_ref[pl.ds(g * NS + sec_ref[0], 1), :]
    for g in range(2):
        hid_out[:, g * LANES : (g + 1) * LANES] = w_hid_ref[:, quarter(g)]
    both_out[0:M, 3 * LANES :] = w_hid_ref[:, quarter(2)]
    both_out[M:, 3 * LANES :] = jnp.zeros((M, LANES), BF)


def events_kernel(sec_ref, ev_ref, pay_ref):
    sec = sec_ref[0]
    block = lax.broadcasted_iota(I32, (SLOTS, 2 * EV), 0) * BR
    lane = lax.broadcasted_iota(I32, (SLOTS, LANES), 1)
    pay = jnp.zeros((SLOTS, LANES), I32)
    for b in range(NS):
        rows = ev_ref[lax.rem(b + NS - sec, NS)]
        to, _, when = message_rows(rows)
        place = to - block
        for r in range(BR):
            latest = jnp.max(jnp.where(place == r, when, 0), axis=1, keepdims=True)
            pay = jnp.where(lane == b * BR + r, latest, pay)
        asked = as_column(rows[6:7, 0:SLOTS])
        pay = jnp.where(lane == PUT + b, jnp.where(asked < 0, BLOCKS, asked), pay)
        pay = jnp.where(lane == GET + b, jnp.where(asked < 0, BLOCKS + 1, asked), pay)
    pay_ref[...] = pay


def owner_kernel(got_ref, last_ref, table_ref, out_ref, rows_ref, table_out, ids_ref, sem):
    got = got_ref[...]
    flipped = jnp.transpose(
        jnp.concatenate([got.astype(F32), jnp.zeros((LANES - SLOTS, LANES), F32)], axis=0)
    ).astype(I32)
    rows_ref[...] = flipped[PUT : PUT + 2 * NS, :]
    scalars = pltpu.make_async_copy(rows_ref, ids_ref, sem)
    scalars.start()
    table_out[:BLOCKS] = table_ref[...]
    table_out[BLOCKS:] = jnp.zeros((8, BR, LANES), BF)
    cand = BLOCKS + NS * SLOTS
    lane = lax.broadcasted_iota(I32, (SLOTS, cand), 1)
    group = lax.broadcasted_iota(I32, (SLOTS, LANES), 1) // BR
    ids_row = jnp.concatenate(
        [lax.broadcasted_iota(I32, (1, BLOCKS), 1)]
        + [flipped[PUT + b : PUT + b + 1, 0:SLOTS] for b in range(NS)],
        axis=1,
    )
    match = jnp.concatenate(
        [
            ((got[:, GET + b : GET + b + 1] == ids_row) & (lane < BLOCKS + SLOTS * b)).astype(F32)
            for b in range(NS)
        ],
        axis=0,
    ).astype(BF)
    base = jnp.concatenate(
        [jnp.zeros((BLOCKS, (NS - 1) * BR), I32), last_ref[...], jnp.zeros((BLOCKS, LANES - NS * BR), I32)],
        axis=1,
    )
    times = jnp.concatenate(
        [base] + [jnp.where(group == b, got, 0) for b in range(NS - 1)] + [jnp.zeros((SLOTS, LANES), I32)],
        axis=0,
    )
    high = jnp.dot(match, (times >> 6).astype(F32).astype(BF), preferred_element_type=F32)
    low = jnp.dot(match, (times & 63).astype(F32).astype(BF), preferred_element_type=F32)
    stamp = high * 64.0 + low
    stamp = jnp.maximum(stamp, pltpu.roll(stamp, LANES - 2 * BR, 1))
    stamp = jnp.maximum(stamp, pltpu.roll(stamp, LANES - BR, 1)).astype(I32)
    total = jnp.zeros((SLOTS, LANES), I32)
    for b in range(NS):
        part = stamp[b * SLOTS : (b + 1) * SLOTS]
        part = pltpu.roll(part, b * BR, 1) if b else part
        total = jnp.where(group == b, part, total)
    packed = (total >> 6) + pltpu.roll(total & 63, PUT, 1)
    spread = jnp.broadcast_to(packed.astype(F32)[:, None, :], (SLOTS, BR, LANES))
    out_ref[:, :, LANES : 2 * LANES] = spread.astype(BF)
    scalars.wait()
    for j in range(SLOTS):
        out_ref[j, :, 0:LANES] = table_out[ids_ref[NS, j]]


def swap_kernel(b, ids_ref, table_ref, back_ref, out_ref, table_out):
    table_out[...] = table_ref[...]
    for j in range(SLOTS):
        table_out[ids_ref[b, j]] = back_ref[j]
    for j in range(SLOTS):
        out_ref[j] = table_out[ids_ref[NS + b + 1, j]]


def cosine(x):
    turns = jnp.round(x * 0.15915494309189535)
    x = x - turns * 6.28125
    x = x - turns * 0.0019340515136718750
    x = x - turns * 1.255665914e-06
    y = x * x
    total = jnp.full_like(y, -1.1470745597729725e-11)
    for c in (
        2.0876756987868099e-09,
        -2.7557319223985893e-07,
        2.4801587301587302e-05,
        -1.3888888888888889e-03,
        4.1666666666666667e-02,
        -0.5,
        1.0,
    ):
        total = total * y + c
    return total


def code_kernel(
    b,
    sec_ref,
    ev_ref,
    stamp_ref,
    rate_ref,
    phase_ref,
    w_code_ref,
    bias_ref,
    out_ref,
    pair_ref,
    share_ref,
):
    rows = ev_ref[lax.rem(b + NS - sec_ref[0], NS)]
    to, other, when = message_rows(rows)
    lane = lax.broadcasted_iota(I32, (ROWS, LANES), 1)
    sub = lax.broadcasted_iota(I32, (ROWS, LANES), 0) & (BR - 1)
    stamps = stamp_ref[:, LANES : 2 * LANES].astype(F32)
    scale = jnp.where(lane == b * BR + sub, 64.0, jnp.where(lane == PUT + b * BR + sub, 1.0, 0.0))
    state_time = jnp.sum(stamps * scale, axis=1, keepdims=True)
    slot = lax.broadcasted_iota(I32, (ROWS, 2 * EV), 0)
    hit = slot == to
    before = jnp.sum(jnp.where(hit, state_time, 0.0), axis=0, keepdims=True)
    delta = when.astype(F32) - before
    code = cosine(as_column(rate_ref[...]) * delta + as_column(phase_ref[...]))
    high = code.astype(BF)
    low = (code - high.astype(F32)).astype(BF)
    hits = hit.astype(F32)
    counts = jnp.sum(hits, axis=1, keepdims=True)
    hits = hits.astype(BF)
    total = lax.dot_general(hits, high, NT, preferred_element_type=F32)
    total = total + lax.dot_general(hits, low, NT, preferred_element_type=F32)
    mean = (total / jnp.maximum(counts, 1.0)).astype(BF)
    out_ref[...] = jnp.dot(mean, w_code_ref[...], preferred_element_type=F32) + bias_ref[...]
    share_ref[...] = jnp.where(counts > 0.0, 1.0 / jnp.maximum(counts, 1.0), 0.0)
    partner = (slot == other).astype(F32).astype(BF)
    pair_ref[...] = lax.dot_general(hits, partner, NT, preferred_element_type=F32).astype(BF)


def cell_kernel(
    b,
    sec_ref,
    own_ref,
    one_ref,
    two_ref,
    three_ref,
    pair_ref,
    code_ref,
    share_ref,
    w_both_ref,
    w_hid_ref,
    *refs,
):
    new_ref, kept_ref, all_ref, sem = refs[-4:]
    sec = sec_ref[0]
    for k, part in enumerate((own_ref, one_ref, two_ref, three_ref)):
        at = pl.multiple_of(lax.rem(sec + k, NS) * LANES, LANES)
        all_ref[:, pl.ds(at, LANES)] = part[...]
    keep = pltpu.make_async_copy(all_ref.at[:, 0:M], kept_ref, sem)

    @pl.when(sec == b)
    def _():
        keep.start()

    share = share_ref[...]
    states = all_ref[:, 0:M]
    trail = jnp.dot(pair_ref[...], states, preferred_element_type=F32) * share
    all_ref[:, M:] = trail.astype(BF)
    both = jnp.dot(all_ref[...], w_both_ref[...], preferred_element_type=F32)
    carried = jnp.dot(states, w_hid_ref[...], preferred_element_type=F32)
    given = code_ref[...]
    gates = both[:, : 2 * LANES] + carried + given[:, : 2 * LANES]
    gates = 0.5 + 0.5 * jnp.tanh(0.5 * gates)
    reset, update = gates[:, :LANES], gates[:, LANES:]
    candidate = both[:, 2 * LANES : 3 * LANES] + given[:, 2 * LANES :]
    candidate = jnp.tanh(candidate + reset * both[:, 3 * LANES :])
    old = own_ref[...].astype(F32)
    new = (1.0 - update) * candidate + update * old
    new_ref[...] = jnp.where(share > 0.0, new, old).astype(BF)

    @pl.when(sec == b)
    def _():
        keep.wait()


def early_kernel(sec_ref, ids_ref, mem_ref, own_ref, one_ref, two_ref, three_ref, out_ref, full_ref, sem):
    sec = sec_ref[0]
    fill = pltpu.make_async_copy(mem_ref, full_ref.at[pl.ds(0, BLOCKS)], sem)
    fill.start()
    fill.wait()
    for b in range(NS - 1):

        @pl.when(sec >= b)
        def _():
            for k, part in enumerate((own_ref, one_ref, two_ref, three_ref)):
                to = pl.multiple_of(lax.rem(sec + k, NS) * LANES, LANES)
                for j in range(SLOTS):
                    full_ref[ids_ref[b, j], :, pl.ds(to, LANES)] = part[b, j]

    drain = pltpu.make_async_copy(full_ref.at[pl.ds(0, BLOCKS)], out_ref, sem)
    drain.start()
    drain.wait()


def late_kernel(sec_ref, ids_ref, zero_ref, one_ref, two_ref, own_ref, early_ref, out_ref, full_ref, sems):
    @pl.when(sec_ref[0] == NS - 1)
    def _():
        for k, part in enumerate((zero_ref, one_ref, two_ref, own_ref)):
            full_ref[:, :, k * LANES : (k + 1) * LANES] = part[...]

        def place(j):
            at = ids_ref[NS - 1, j]
            return at, pltpu.make_async_copy(
                full_ref.at[j], out_ref.at[jnp.minimum(at, BLOCKS - 1)], sems.at[j]
            )

        for j in range(SLOTS):
            at, copy = place(j)

            @pl.when(at < BLOCKS)
            def _():
                copy.start()

        for j in range(SLOTS):
            at, copy = place(j)

            @pl.when(at < BLOCKS)
            def _():
                copy.wait()


def embed_kernel(source_ref, near_ref, kept_ref, weight_ref, out_ref):
    slot = lax.broadcasted_iota(I32, (EV, ROWS), 1)
    block = slot >> 3
    picks = jnp.zeros((EV, ROWS), F32)
    for k in range(near_ref.shape[0]):
        picks = picks + jnp.where(block == as_column(near_ref[k : k + 1, :]), 1.0 / BR, 0.0)
    states = kept_ref[...]
    near = jnp.dot(picks.astype(BF), states, preferred_element_type=F32).astype(BF)
    mixed = jnp.dot(near, weight_ref[...], preferred_element_type=F32)
    own = (slot == as_column(source_ref[...])).astype(F32).astype(BF)
    out_ref[...] = (jnp.dot(own, states, preferred_element_type=F32) + mixed).astype(BF)


def from_sections(array):
    return [array] + [
        lax.ppermute(array, "section", [(i, (i - k) % NS) for i in range(NS)]) for k in range(1, NS)
    ]


def exchange(array):
    return lax.all_to_all(array, "shard", split_axis=0, concat_axis=0, tiled=True)


def on_device(
    memory,
    last_time,
    requests,
    event_source,
    event_target,
    event_time,
    neighbour_blocks,
    time_rates,
    time_phase,
    w_input,
    w_hidden,
    bias_input,
    w_neighbour,
):
    sec = lax.axis_index("section")
    sec_ref = sec.astype(I32).reshape(1)
    source = event_source[0]
    ints = jnp.concatenate(
        [
            source,
            event_target[0],
            event_time[0],
            requests.reshape(SLOTS),
            jnp.zeros((8 * LANES - 3 * EV - SLOTS,), I32),
        ]
    ).reshape(8, LANES)
    parts = from_sections(ints)
    table = lax.dynamic_slice_in_dim(memory, sec * LANES, LANES, axis=1)
    last = last_time.reshape(BLOCKS, BR)
    bias_row = bias_input.reshape(3 * NS, LANES)
    parts, table, last, bias_row = lax.optimization_barrier((parts, table, last, bias_row))
    events = jnp.stack(parts)
    pay = call(
        events_kernel, jax.ShapeDtypeStruct((SLOTS, LANES), I32), (SMEM, VMEM), moved=10**6
    )(sec_ref, events)
    ids = exchange(pay.reshape(SLOTS, 1, LANES)).reshape(SLOTS, LANES)
    picked, ids, table = call(
        owner_kernel,
        (
            jax.ShapeDtypeStruct((SLOTS, BR, 2 * LANES), BF),
            jax.ShapeDtypeStruct((2 * NS, LANES), I32),
            jax.ShapeDtypeStruct((BLOCKS + 8, BR, LANES), BF),
        ),
        (VMEM, VMEM, VMEM),
        scratch=(pltpu.SMEM((2 * NS, LANES), I32), pltpu.SemaphoreType.DMA),
        moved=10**6,
    )(ids, last, table.reshape(BLOCKS, BR, LANES))
    stamps = kept = None
    backs = []
    for b in range(NS):
        pulled = exchange(picked).reshape(ROWS, -1)
        if b == 0:
            stamps = pulled
            pulled = pulled[:, :LANES]
            pulled, later = lax.optimization_barrier((pulled, sec_ref))
            w_both, w_hid, w_code, bias = call(
                prep_kernel,
                (
                    jax.ShapeDtypeStruct((2 * M, 4 * LANES), BF),
                    jax.ShapeDtypeStruct((M, 2 * LANES), BF),
                    jax.ShapeDtypeStruct((LANES, 3 * LANES), BF),
                    jax.ShapeDtypeStruct((1, 3 * LANES), F32),
                ),
                (SMEM, VMEM, VMEM, VMEM),
                moved=3 * 10**6,
            )(later, w_input, w_hidden, bias_row)
        if b == NS - 1:
            early = from_sections(jnp.stack(backs))
            pulled, early[1] = lax.optimization_barrier((pulled, early[1]))
        parts = from_sections(pulled)
        if b == NS - 1:
            full = jax.ShapeDtypeStruct((BLOCKS, BR, M), BF)
            final = call(
                early_kernel,
                full,
                (SMEM, SMEM, pl.ANY) + (VMEM,) * NS,
                to=spec(pl.ANY),
                scratch=(pltpu.VMEM((BLOCKS + 8, BR, M), BF), pltpu.SemaphoreType.DMA),
                moved=8 * 10**6,
            )(sec_ref, ids, memory.reshape(BLOCKS, BR, M), *early)
            parts, final = lax.optimization_barrier((parts, final))
        code, pairs, share = call(
            functools.partial(code_kernel, b),
            (
                jax.ShapeDtypeStruct((ROWS, 3 * LANES), F32),
                jax.ShapeDtypeStruct((ROWS, ROWS), BF),
                jax.ShapeDtypeStruct((ROWS, 1), F32),
            ),
            (SMEM,) + (VMEM,) * 6,
            flops=2 * ROWS**3,
            moved=10**6,
        )(
            sec_ref,
            events,
            stamps,
            time_rates.reshape(1, LANES),
            time_phase.reshape(1, LANES),
            w_code,
            bias,
        )
        updated, kept = call(
            functools.partial(cell_kernel, b),
            (jax.ShapeDtypeStruct((ROWS, LANES), BF), jax.ShapeDtypeStruct((ROWS, M), BF)),
            (SMEM,) + (VMEM,) * 9 + ((pl.ANY,) if b else ()),
            to=(spec(), spec(pl.ANY)),
            scratch=(pltpu.VMEM((ROWS, 2 * M), BF), pltpu.SemaphoreType.DMA),
            flops=2 * ROWS * M * (M + 9 * LANES),
            moved=4 * 10**6,
            aliases={10: 1} if b else None,
        )(sec_ref, *parts, pairs, code, share, w_both, w_hid, *([kept] if b else []))
        updated = updated.reshape(SLOTS, BR, LANES)
        if b == NS - 1:
            updated, near, source = lax.optimization_barrier(
                (updated, neighbour_blocks[0].T, source)
            )
        back = exchange(updated)
        if b < NS - 1:
            backs.append(back)
            block = jax.ShapeDtypeStruct((SLOTS, BR, LANES), BF)
            whole = (BLOCKS + 8, BR, LANES)
            if b < NS - 2:
                picked, table = call(
                    functools.partial(swap_kernel, b),
                    (block, jax.ShapeDtypeStruct(whole, BF)),
                    (SMEM, VMEM, VMEM),
                    moved=10**6,
                )(ids, table, back)
            else:
                picked = call(
                    functools.partial(swap_kernel, b),
                    block,
                    (SMEM, VMEM, VMEM),
                    scratch=(pltpu.VMEM(whole, BF),),
                    moved=10**6,
                )(ids, table, back)

    late = [lax.ppermute(back, "section", [(k, NS - 1)]) for k in range(NS - 1)]
    final = call(
        late_kernel,
        full,
        (SMEM, SMEM) + (VMEM,) * NS + (pl.ANY,),
        to=spec(pl.ANY),
        scratch=(pltpu.VMEM((SLOTS, BR, M), BF), pltpu.SemaphoreType.DMA((SLOTS,))),
        moved=10**6,
        aliases={6: 0},
    )(sec_ref, ids, *late, back, final)

    embedded = call(
        embed_kernel,
        jax.ShapeDtypeStruct((EV, M), BF),
        (VMEM,) * 4,
        flops=2 * EV * M * (2 * ROWS + M),
        moved=10**6,
    )(source.reshape(1, EV), near, kept, w_neighbour)
    return (final.reshape(1, BLOCKS * BR, M), embedded[None])


def solution(mesh):
    return jax.shard_map(
        on_device,
        mesh=mesh,
        in_specs=(
            P("shard", None),
            P("shard"),
            P("section", "shard", None, None),
            P("section", "shard"),
            P("section", "shard"),
            P("section", "shard"),
            P("section", "shard", None),
            P(),
            P(),
            P(),
            P(),
            P(),
            P(),
        ),
        out_specs=(P("section", "shard", None), P("section", "shard", None)),
        check_vma=False,
    )
```
